512 devices in a mesh: dp: 64 (over z, y), table: 8 (over x, core).
Axes of the slice: x: 4, y: 4, z: 16, core: 2. Of those that a mesh axis runs over, the one named last changes fastest.
Arguments:
- token_slot: int32 [2, 512, 256], P(None, ('dp', 'table')), may hold values from 0 to 127, as said below
- seg_ids: int32 [2, 512, 256], P(None, ('dp', 'table')), may hold values from 0 to 3, never falling along the last dimension, each value on 1 to 128 neighbouring positions
- req_rows: int32 [2, 4096, 16], P(None, ('dp', 'table')), may hold values from 0 to 127, as said below
- cotangent: bfloat16 [2, 131072, 512], P(None, ('dp', 'table')), may hold values from -6 to 6
- uvqk_weight: bfloat16 [1024, 2048], P('dp'), may hold values from -0.1875 to 0.1875
- table: bfloat16 [1024, 1024], P('table'), may hold values from -6 to 6
- first_moment: float32 [1024, 1024], P('table'), may hold values from -6 to 6
- second_moment: float32 [1024, 1024], P('table'), may hold values from 0.1 to 1
- dup_count: int32 [64], replicated, may hold values from 0 to 8, as said below
- dup_target: int32 [64, 8], replicated, may hold values from 0 to 63
Outputs:
- new_rows: bfloat16 [1024, 1024], P('table')
- new_first: float32 [1024, 1024], P('table')
- new_second: float32 [1024, 1024], P('table')
The draws below stay inside these ranges and needn't reach their ends.
Inputs may be any that keep to these rules, and one draw needn't show every extreme that they name: `token_slot`: every one of a device's 8 * 16 slots holds some token in each micro-step. `req_rows`: the 16 requests of one device to one shard in one micro-step are distinct rows. `dup_count`: each shard has exactly 8 live replicas for some owner shard, which may be itself.
All inputs are finite; a program needn't handle non-finite values.
Results may differ from the reference program's by a relative error of at most 0.014.
Values may be sent and summed in bfloat16 or wider, within the bound.
A program may use at most 64 MiB of HBM per device.

```python
import math
import jax
import jax.numpy as jnp
import numpy as np
from jax import lax

D = 1024
HEADS = 4
HD = 512
TOK_DEV = 256
USERS = 4
MAXLEN = 128
CAP = 16
MICRO = 2
HOT_DEV = 128
DCAP = 8
OWN = 64
HOT_ROWS = 1024
TOKENS = 131072
N_TABLE = 8
DEVICES = 512


def draw_token_slot(key, part):
    key = jax.random.fold_in(key, 11)
    first_key, second_key = jax.random.split(key)
    live = N_TABLE * CAP
    place = jnp.arange(TOK_DEV, dtype=jnp.int32)
    extra = jax.random.randint(first_key, (MICRO, DEVICES, TOK_DEV), 0, live, dtype=jnp.int32)
    base = jnp.where(place[None, None, :] < live, place[None, None, :], extra)
    row_keys = jax.random.split(second_key, MICRO * DEVICES)
    orders = jax.vmap(lambda single: jax.random.permutation(single, TOK_DEV))(row_keys).reshape(MICRO, DEVICES, TOK_DEV)
    return jnp.take_along_axis(base, orders.astype(jnp.int32), axis=2).astype(jnp.int32)


def draw_req_rows(key, part):
    key = jax.random.fold_in(key, 37)
    first_key, second_key, third_key = jax.random.split(key, 3)
    groups = MICRO * DEVICES * N_TABLE
    row_keys = jax.random.split(first_key, groups)
    picks = jax.vmap(lambda single: jax.random.permutation(single, HOT_DEV)[:CAP])(row_keys)
    picks = picks.reshape(MICRO, DEVICES * N_TABLE, CAP).astype(jnp.int32)
    middle = 1 + jax.random.permutation(second_key, HOT_DEV - 2)[:CAP - 2].astype(jnp.int32)
    planted = jnp.concatenate([jnp.array([0, HOT_DEV - 1], jnp.int32), middle])
    planted = jax.random.permutation(third_key, planted).astype(jnp.int32)
    picks = picks.at[:, 0, :].set(jnp.broadcast_to(planted[None, :], (MICRO, CAP)))
    return picks.astype(jnp.int32)


def draw_dup_count(key, part):
    key = jax.random.fold_in(key, 23)
    first_key, second_key = jax.random.split(key)
    counts = jax.random.randint(first_key, (N_TABLE, N_TABLE), 0, DCAP + 1, dtype=jnp.int32)
    fullest = jax.random.randint(second_key, (N_TABLE,), 0, N_TABLE, dtype=jnp.int32)
    owners = jnp.arange(N_TABLE, dtype=jnp.int32)
    counts = jnp.where(owners[None, :] == fullest[:, None], DCAP, counts)
    return counts.reshape(-1).astype(jnp.int32)


def plant(result, rng, smallest, largest):
    longest = result.shape.index(max(result.shape))
    spots = []
    for shift in (0, 1):
        where = [jax.random.randint(jax.random.fold_in(rng, axis), (), 0, length) for axis, length in enumerate(result.shape)]
        where[longest] = (where[longest] + shift) % result.shape[longest]
        spots.append(tuple(where))
    return result.at[spots[0]].set(smallest).at[spots[1]].set(largest)


def shard_levels(rng, extent, cuts, low, largest):
    def one(position, parts):
        draws = jax.random.uniform(jax.random.fold_in(jax.random.fold_in(rng, 6), position), (parts,), jnp.float32, low / len(cuts), largest / len(cuts))
        return jnp.repeat(jnp.exp(draws), extent[position] // parts).reshape((-1,) + (1,) * (len(extent) - position - 1))

    loudness = one(*cuts[0])
    for cut in cuts[1:]:
        loudness = loudness * one(*cut)
    return loudness


def profile(number_of, total, most, skew):
    portions = [(1 << 20) // math.isqrt(grade ** skew) + 1 for grade in range(2, number_of + 1)]
    surplus, given = total - most - (number_of - 1), [1] * (number_of - 1)
    while surplus > 0:
        movable = [i for i in range(number_of - 1) if given[i] < most]
        pool, left = sum([portions[i] for i in movable]), surplus
        for i in movable:
            addition = min(most - given[i], max(1, left * portions[i] // pool), surplus)
            given[i] = given[i] + addition
            surplus = surplus - addition
    return np.array([most] + given)


def uneven(own_key, count, total, reach, lean):
    if count == 2:
        one = jax.random.randint(own_key, (), max(1, total - reach), min(reach, total - 1) + 1)
        return jnp.stack([one, total - one])
    tallies = jnp.asarray(profile(count, total, reach, lean), jnp.int32)
    pairs = (count - 1) // 2
    giver, receiver = tallies[1:1 + 2 * pairs:2], tallies[2:2 + 2 * pairs:2]
    slack = jnp.minimum(giver - 1, reach - receiver)
    moved = jax.random.randint(jax.random.fold_in(own_key, 1), (pairs,), 0, 1 << 20) % (slack + 1)
    tallies = tallies.at[1:1 + 2 * pairs:2].set(giver - moved).at[2:2 + 2 * pairs:2].set(receiver + moved)
    return tallies[jax.random.permutation(jax.random.fold_in(own_key, 2), count)]


def centred(own_key, shape, scale, limit, cuts=(), kind=jnp.bfloat16):
    values = jax.random.normal(own_key, shape, jnp.float32) * scale
    if len(cuts) > 0:
        values = shard_levels(own_key, shape, cuts, -0.22, 0.18) * values
    return jnp.clip(values, min=-limit, max=limit).astype(kind)


def setup_inputs(seed: int = 0) -> dict:
    splits = jax.random.split(jax.random.key(seed), 11)
    token_slot = draw_token_slot(jax.random.fold_in(splits[10], 71), 0)
    seg_ids = jax.vmap(lambda own: jnp.searchsorted(jnp.cumsum(uneven(own, USERS, TOK_DEV, MAXLEN, 2)), jnp.arange(TOK_DEV), side="right"))(jax.random.split(splits[1], MICRO * DEVICES)).reshape((MICRO, DEVICES, TOK_DEV)).astype(jnp.int32)
    req_rows = draw_req_rows(jax.random.fold_in(splits[10], 71), 0)
    cotangent = centred(splits[3], (MICRO, TOKENS, HD), 1.0, 6.0, ((1, 512),))
    uvqk_weight = centred(splits[4], (D, 4 * HD), D ** -0.5, 0.1875, ((0, 64),))
    table = centred(splits[5], (HOT_ROWS, D), 1.0, 6.0, ((0, 8),))
    first_moment = centred(splits[6], (HOT_ROWS, D), 1.0, 6.0, ((0, 8),), jnp.float32)
    second_moment = jnp.clip(jnp.exp(math.log(1.0) - 2.3025851 * jax.random.uniform(splits[7], (HOT_ROWS, D), jnp.float32) ** shard_levels(splits[7], (HOT_ROWS, D), ((0, 8),), -0.2, 0.2)), 0.1, 1.0)
    dup_count = draw_dup_count(jax.random.fold_in(splits[10], 71), 0)
    dup_target = plant(jax.random.randint(splits[9], (N_TABLE * N_TABLE, DCAP), 0, OWN), jax.random.fold_in(splits[9], 1), 0, OWN - 1).astype(jnp.int32)
    return {"token_slot": token_slot, "seg_ids": seg_ids, "req_rows": req_rows, "cotangent": cotangent, "uvqk_weight": uvqk_weight, "table": table, "first_moment": first_moment, "second_moment": second_moment, "dup_count": dup_count, "dup_target": dup_target}


beta_one = 0.9
beta_two = 0.999
learn_rate = 0.1
adam_eps = 1e-08
norm_eps = 1e-05

def layer_norm(values):
    center = lax.optimization_barrier(jnp.mean(values, axis=-1, keepdims=True))
    shifted = values - center
    spread = lax.optimization_barrier(jnp.mean(shifted * shifted, axis=-1, keepdims=True))
    return shifted * lax.rsqrt(spread + norm_eps)

def hstu_block(inputs, weight, segment, heads):
    normed = layer_norm(inputs).astype(jnp.bfloat16)
    projected = jax.nn.silu(jnp.dot(normed, weight, preferred_element_type=jnp.float32))
    width = weight.shape[1] // 4
    count = inputs.shape[0]
    head_dim = width // heads
    gate = projected[:, :width]
    values = projected[:, width:2 * width].astype(jnp.bfloat16).reshape(count, heads, head_dim)
    queries = projected[:, 2 * width:3 * width].astype(jnp.bfloat16).reshape(count, heads, head_dim)
    keys_part = projected[:, 3 * width:].astype(jnp.bfloat16).reshape(count, heads, head_dim)
    scores = jnp.einsum('thd,shd->hts', queries, keys_part, preferred_element_type=jnp.float32) * head_dim ** (-0.5)
    same = segment[:, None] == segment[None, :]
    place = jnp.arange(count, dtype=jnp.int32)
    causal = place[:, None] >= place[None, :]
    masked = jnp.where(same & causal, 1.0, 0.0).astype(jnp.float32)
    history = lax.optimization_barrier(jnp.sum(jnp.where(same, 1.0, 0.0).astype(jnp.float32), axis=1))
    attn = (jax.nn.silu(scores) * masked[None] / history[None, :, None]).astype(jnp.bfloat16)
    mixed = jnp.einsum('hts,shd->thd', attn, values, preferred_element_type=jnp.float32).reshape(count, width)
    return layer_norm(mixed) * gate

def reference(token_slot, seg_ids, req_rows, cotangent, uvqk_weight, table, first_moment, second_moment, dup_count, dup_target):
    shards = N_TABLE
    owned = HOT_DEV - shards * DCAP
    total = jnp.zeros((shards * HOT_DEV, D), jnp.float32)
    shard_base = (jnp.arange(shards, dtype=jnp.int32) * HOT_DEV)[:, None]

    def device_step(carry, data):
        slots, segment, requests, upstream = data
        rows = (shard_base + requests).reshape(-1).astype(jnp.int32)
        fetched = table[rows]
        inputs = fetched[slots].astype(jnp.float32)
        _, pullback = jax.vjp(lambda given: hstu_block(given, uvqk_weight, segment, HEADS), inputs)
        grad_inputs = pullback(upstream.astype(jnp.float32))[0]
        slot_grad = jax.ops.segment_sum(grad_inputs, slots, num_segments=shards * CAP)
        return (carry + jax.ops.segment_sum(slot_grad, rows, num_segments=shards * HOT_DEV), None)
    for micro in range(MICRO):
        data = (token_slot[micro], seg_ids[micro], req_rows[micro].reshape(DEVICES, shards, CAP), cotangent[micro].reshape(DEVICES, TOK_DEV, HD))
        total, _ = lax.scan(device_step, total, data)
    first_step = beta_one * first_moment + (1.0 - beta_one) * total
    second_step = beta_two * second_moment + (1.0 - beta_two) * total * total
    counts = dup_count.reshape(shards, shards)
    place = jnp.arange(DCAP, dtype=jnp.int32)
    live = place[None, None, :] < counts[:, :, None]
    livef = jnp.where(live, 1.0, 0.0).astype(jnp.float32)
    targets = (dup_target.reshape(shards, shards, DCAP) + shard_base[None, :, :]).reshape(-1).astype(jnp.int32)
    rep_first = first_step.reshape(shards, HOT_DEV, D)[:, owned:].reshape(shards, shards, DCAP, D)
    rep_second = second_step.reshape(shards, HOT_DEV, D)[:, owned:].reshape(shards, shards, DCAP, D)
    add_first = jax.ops.segment_sum((rep_first * livef[..., None]).reshape(-1, D), targets, num_segments=shards * HOT_DEV)
    add_second = jax.ops.segment_sum((rep_second * livef[..., None]).reshape(-1, D), targets, num_segments=shards * HOT_DEV)
    tally = jax.ops.segment_sum(livef.reshape(-1), targets, num_segments=shards * HOT_DEV)
    replica = jnp.concatenate([jnp.zeros((shards, owned), jnp.bool_), live.reshape(shards, shards * DCAP)], axis=1).reshape(-1)
    scale = 1.0 / (1.0 + tally)
    new_first = jnp.where(replica[:, None], 0.0, (first_step + add_first) * scale[:, None])
    new_second = jnp.where(replica[:, None], 0.0, (second_step + add_second) * scale[:, None])
    update = table.astype(jnp.float32) - learn_rate * new_first / (jnp.sqrt(new_second) + adam_eps)
    new_rows = jnp.where(replica[:, None], 0.0, update).astype(jnp.bfloat16)
    return (new_rows, new_first, new_second)
```

```python
import functools

import jax
import jax.numpy as jnp
from jax import lax
from jax.experimental import pallas as pl
from jax.experimental.pallas import tpu as pltpu
from jax.sharding import PartitionSpec as P

MESH = pl.DeviceIdType.MESH
HEADS = 4
MICRO = 2
NX = 4
NY = 4
SHARDS = 8
CAP = 16
DCAP = 8

beta_one = 0.9
beta_two = 0.999
learn_rate = 0.1
adam_eps = 1e-08
norm_eps = 1e-05


def dot(a, b, dims=((1,), (0,))):
    return lax.dot_general(a, b, (dims, ((), ())), preferred_element_type=jnp.float32)


def place():
    dp = lax.axis_index("dp")
    shard = lax.axis_index("table")
    return dp // NY, dp % NY, shard // 2, shard % 2, dp, shard


def greet(peers):
    barrier = pltpu.get_barrier_semaphore()
    for peer in peers:
        pl.semaphore_signal(barrier, inc=1, device_id=peer, device_id_type=MESH)
    pl.semaphore_wait(barrier, len(peers))


def remote(src, dst, send, recv, peer):
    return pltpu.make_async_remote_copy(
        src_ref=src, dst_ref=dst, send_sem=send, recv_sem=recv, device_id=peer, device_id_type=MESH
    )


def slot_rows(held_ref, group):
    rows = held_ref[4 * group]
    for peer in range(1, 4):
        rows = jnp.maximum(rows, held_ref[4 * group + peer])
    number = lax.broadcasted_iota(jnp.int32, (128, 128), 0)
    return jnp.where(number == rows[0:1], 1.0, 0.0).astype(jnp.bfloat16)


def normalise(values):
    center = jnp.mean(values, axis=-1, keepdims=True)
    shifted = values - center
    spread = jnp.mean(shifted * shifted, axis=-1, keepdims=True)
    factor = lax.rsqrt(spread + norm_eps)
    return shifted * factor, factor


def normalise_back(grad, normed, factor):
    grad_mean = jnp.mean(grad, axis=-1, keepdims=True)
    along = jnp.mean(grad * normed, axis=-1, keepdims=True)
    return factor * (grad - grad_mean - normed * along)


def sigmoid(values):
    return 0.5 * jnp.tanh(0.5 * values) + 0.5


def whole_kernel(
    nz,
    req_hbm,
    slot_hbm,
    seg_hbm,
    tally_hbm,
    target_hbm,
    table_hbm,
    w_hbm,
    cot_hbm,
    first_hbm,
    second_hbm,
    first_out,
    second_out,
    req_ref,
    slot_ref,
    seg_ref,
    tally_ref,
    target_ref,
    asked,
    held,
    table_ref,
    wout,
    cot_ref,
    first_ref,
    second_ref,
    found,
    fetched,
    slope,
    flow,
    attn,
    attn_slope,
    mixed,
    back,
    grads,
    arrived,
    y_send,
    y_got,
    z_send,
    z_got,
    total,
    mom_send,
    mom_got,
    rep_send,
    rep_got,
    local_s,
    req_s,
    req_r,
    fnd_s,
    fnd_r,
    z_s,
    z_r,
    ring_s,
    ring_r,
    core_s,
    core_r,
    a_s,
    a_r,
    ry_s,
    ry_r,
    rz_s,
    rz_r,
    gz_s,
    gz_r,
    gy_s,
    gy_r,
    m_s,
    m_r,
    r_s,
    r_r,
):
    z, y, x, core, dp, shard = place()
    other = 1 - core
    half = nz // 2
    columns = table_ref.shape[1]
    blocks = columns // 128
    f32, bf16 = jnp.float32, jnp.bfloat16

    def table_peer(k):
        return lax.rem(shard + k, SHARDS)

    def z_peer(k):
        return lax.rem(z + k, nz)

    def y_peer(k):
        return lax.rem(y + k, NY)

    def along_y(k):
        return (z * NY + y_peer(k), shard)

    def along_x(k):
        return (dp, lax.rem(x + k, NX) * 2 + core)

    across_table = (4, 3, 5, 2, 6, 1, 7)
    across_z = [nz // 2]
    for k in range(nz // 2 - 1, 0, -1):
        across_z += [k, nz - k]
    across_y = (2, 1, 3)

    local = [(req_hbm, req_ref)]
    for g in range(2):
        part = pl.ds(pl.multiple_of(shard * 256 + g * 128, 128), 128)
        local.append((w_hbm.at[:, part], wout.at[x, core, g, z, y]))
    local += [
        (table_hbm, table_ref),
        (cot_hbm, cot_ref),
        (first_hbm, first_ref),
        (second_hbm, second_ref),
        (slot_hbm, slot_ref),
        (seg_hbm, seg_ref),
        (tally_hbm, tally_ref),
        (target_hbm, target_ref),
    ]
    local = [pltpu.make_async_copy(a, b, local_s.at[i]) for i, (a, b) in enumerate(local)]
    for copy in local:
        copy.start()

    local[0].wait()
    lane = lax.broadcasted_iota(jnp.int32, (CAP, 128), 1) % 32
    deep = lax.broadcasted_iota(jnp.int32, (CAP, 128), 0)
    wide = jnp.zeros((SHARDS, 128), f32)
    for m in range(MICRO):
        spot = jnp.where(lane == deep + m * CAP, 1.0, 0.0).astype(bf16)
        wide = wide + dot(req_ref[m].astype(f32).astype(bf16), spot)
    mine = lax.broadcasted_iota(jnp.int32, (SHARDS, 128), 1) // 32 == lax.rem(shard, 4)
    wide = jnp.where(mine, wide.astype(jnp.int32), -1)
    for p in range(SHARDS):
        asked[p] = jnp.broadcast_to(wide[p : p + 1], (8, 128))

    greet(
        [(dp, table_peer(k)) for k in range(1, SHARDS)]
        + [(z_peer(k) * NY + y, shard) for k in range(1, nz)]
        + [along_y(k) for k in range(1, NY)]
    )

    started = []

    def start(copy):
        copy.start()
        started.append(copy)
        return copy

    for k in across_table:
        p = table_peer(k)
        start(remote(asked.at[p], held.at[shard], req_s.at[k], req_r.at[shard], (dp, p)))
    held[shard] = asked[shard]

    local[1].wait()
    local[2].wait()
    for k in across_z:
        q = z_peer(k)
        block = wout.at[x, core, :, z, y]
        start(remote(block, block, z_s.at[k], z_r.at[z], (q * NY + y, shard)))

    local[3].wait()
    for k in reversed(across_table):
        p = table_peer(k)
        remote(asked.at[p], held.at[p], req_s.at[k], req_r.at[p], (dp, p)).wait_recv()
    for group in range(2):
        rows = dot(slot_rows(held, group), table_ref[...], ((0,), (0,)))
        found[4 * group : 4 * group + 4] = rows.astype(bf16).reshape(4, MICRO, CAP, columns)
    for k in across_table:
        p = table_peer(k)
        start(remote(found.at[p], fetched.at[shard], fnd_s.at[k], fnd_r.at[shard], (dp, p)))
    fetched[shard] = found[shard]

    for k in reversed(across_z):
        q = z_peer(k)
        block = wout.at[x, core, :, q, y]
        remote(block, block, z_s.at[k], z_r.at[q], (q * NY + y, shard)).wait_recv()

    whole, low, high = pl.ds(0, nz), pl.ds(0, half), pl.ds(half, half)
    views = (
        lambda i, zs: wout.at[x, core, 0, zs, i],
        lambda i, zs: wout.at[i, core, 1, zs, y],
        lambda i, zs: wout.at[i, core, 0, zs],
        lambda i, zs: wout.at[:, core, 1, zs, i],
    )
    spots = (y, x, x, y)
    steps = (along_y, along_x, along_x, along_y)

    def link(ring, which, offset, zs, to):
        block = views[ring](lax.rem(spots[ring] + offset, 4), zs)
        return remote(
            block, block, ring_s.at[ring, which], ring_r.at[ring, which], steps[ring](to)
        )

    def ring_first(ring):
        start(link(ring, 0, 0, whole, 1))
        start(link(ring, 1, 0, whole, 3))

    def ring_second(ring):
        link(ring, 0, 3, whole, 1).wait_recv()
        start(link(ring, 2, 3, low, 1))
        link(ring, 1, 1, whole, 3).wait_recv()
        start(link(ring, 3, 1, high, 3))

    def ring_third(ring):
        link(ring, 2, 2, low, 1).wait_recv()
        link(ring, 3, 2, high, 3).wait_recv()

    def across(ring, offset, mine=True):
        i = lax.rem(spots[ring] + offset, 4)
        c = core if mine else other
        block = wout.at[i, c, 0] if ring == 2 else wout.at[:, c, 1, :, i]
        s = (ring - 2) * 4 + offset
        return remote(block, block, core_s.at[s], core_r.at[s], (dp, x * 2 + other))

    for ring in (0, 1):
        ring_first(ring)
    for ring in (0, 1):
        ring_second(ring)
    for ring in (0, 1):
        ring_third(ring)
    for ring in (2, 3):
        ring_first(ring)
        start(across(ring, 0))

    for k in reversed(across_table):
        p = table_peer(k)
        remote(found.at[p], fetched.at[p], fnd_s.at[k], fnd_r.at[p], (dp, p)).wait_recv()
    for copy in local[7:]:
        copy.wait()
    count = seg_ref.shape[2]
    slots = SHARDS * CAP
    collect, expand, share = [], [], []
    number = lax.broadcasted_iota(jnp.int32, (slots, count), 0)
    user = lax.broadcasted_iota(jnp.int32, (8, count), 0)
    causal = lax.broadcasted_iota(jnp.int32, (count, count), 0) >= lax.broadcasted_iota(
        jnp.int32, (count, count), 1
    )
    for m in range(MICRO):
        hot = jnp.where(number == slot_ref[m], 1.0, 0.0)
        collect.append(hot.astype(bf16))
        expand.append(jnp.transpose(hot).astype(bf16))
        belongs = jnp.where(user == seg_ref[m], 1.0, 0.0).astype(bf16)
        same = dot(belongs, belongs, ((0,), (0,)))
        history = jnp.sum(same, axis=1, keepdims=True)
        share.append(jnp.where(causal, same, 0.0) / history)
    rows = jnp.concatenate(
        [fetched[:, m].reshape(slots, columns) for m in range(MICRO)], axis=0
    ).astype(f32)
    normed, factor = normalise(rows)
    given = normed.astype(bf16)

    i32 = jnp.int32
    live = lax.broadcasted_iota(i32, (DCAP, 64), 0) < tally_ref[...]
    aims = jnp.where(live, target_ref[...] + 1, 0).astype(f32).astype(bf16)
    lane = lax.broadcasted_iota(i32, (64, 64), 1)
    deep = lax.broadcasted_iota(i32, (64, 64), 0)
    here = jnp.where(deep == (lane // DCAP) * SHARDS + shard, 1.0, 0.0).astype(bf16)
    aims = dot(aims, here)
    lane = lax.broadcasted_iota(i32, (DCAP, 64), 1) % DCAP
    deep = lax.broadcasted_iota(i32, (DCAP, 64), 0)
    aims = jnp.sum(jnp.where(lane == deep, aims, 0.0), axis=0, keepdims=True).astype(i32) - 1
    number = lax.broadcasted_iota(i32, (128, 64), 0)
    pick = jnp.where(number == aims, 1.0, 0.0)
    tally = jnp.sum(pick, axis=1, keepdims=True)
    pick = pick.astype(bf16)
    lane = lax.broadcasted_iota(i32, (64, 64), 1)
    deep = lax.broadcasted_iota(i32, (64, 64), 0)
    limit = jnp.where(lane == shard * SHARDS + deep // DCAP, tally_ref[...].astype(f32), 0.0)
    limit = jnp.sum(limit, axis=1, keepdims=True)
    row = (lax.broadcasted_iota(i32, (64, 1), 0) % DCAP).astype(f32)
    scale = 1.0 / (1.0 + tally)
    scale = jnp.concatenate([scale[:64], jnp.where(row < limit, 0.0, scale[64:])], axis=0)

    for ring in (2, 3):
        ring_second(ring)
        start(across(ring, 3))
        start(across(ring, 1))
    for ring in (2, 3):
        ring_third(ring)
        start(across(ring, 2))

    for copy in local[4:7]:
        copy.wait()
    for p in range(SHARDS):
        line = slice(64 + DCAP * p, 64 + DCAP * p + DCAP)
        mom_send[p] = jnp.concatenate([first_ref[line], second_ref[line]], axis=0).astype(bf16)
    for ring in (2, 3):
        for offset in (0, 3, 1, 2):
            across(ring, offset, mine=False).wait_recv()
    for k in across_table:
        p = table_peer(k)
        start(remote(mom_send.at[p], mom_got.at[shard], m_s.at[k], m_r.at[shard], (dp, p)))
    mom_got[shard] = mom_send[shard]

    width = 512
    head = width // HEADS

    def weight(i):
        sides = [wout[i // 2, i % 2, g].reshape(columns, 128) for g in range(2)]
        return jnp.concatenate(sides, axis=1)

    for i in range(8):
        flat = dot(given, weight(i))
        sig = sigmoid(flat)
        value = flat * sig
        slope[:, 256 * i : 256 * i + 256] = sig * (1.0 + flat * (1.0 - sig))
        top = value.astype(bf16)
        for m in range(MICRO):
            span = slice(m * count, (m + 1) * count)
            part = slice(m * slots, (m + 1) * slots)
            spread = dot(expand[m], top[part])
            flow[span, 256 * i : 256 * i + 256] = spread.astype(bf16)

    def slot_send(piece, src, to, k, p):
        m = min(piece, 1)
        over = slice(None) if piece == 0 else pl.ds((piece - 1) * columns // 2, columns // 2)
        return remote(
            grads.at[src, m, :, over],
            arrived.at[to, m, :, over],
            a_s.at[piece, k],
            a_r.at[piece, to],
            (dp, p),
        )

    factor_scale = head ** (-0.5)
    for m in range(MICRO):
        span = slice(m * count, (m + 1) * count)
        part = slice(m * slots, (m + 1) * slots)
        for h in range(HEADS):
            values = flow[span, width + h * head : width + (h + 1) * head]
            queries = flow[span, 2 * width + h * head : 2 * width + (h + 1) * head]
            keys = flow[span, 3 * width + h * head : 3 * width + (h + 1) * head]
            scores = dot(queries, keys, ((1,), (1,))) * factor_scale
            sig = sigmoid(scores)
            shared = share[m] * sig
            weights = (scores * shared).astype(bf16)
            attn[h] = weights
            attn_slope[h] = shared * (1.0 + scores * (1.0 - sig)) * factor_scale
            mixed[:, h * head : (h + 1) * head] = dot(weights, values)
        level, spread = normalise(mixed[...])
        upstream = cot_ref[m].astype(f32)
        back[:, :width] = (upstream * level).astype(bf16)
        grad_mixed = normalise_back(
            upstream * flow[span, :width].astype(f32), level, spread
        ).astype(bf16)
        for h in range(HEADS):
            values = flow[span, width + h * head : width + (h + 1) * head]
            queries = flow[span, 2 * width + h * head : 2 * width + (h + 1) * head]
            keys = flow[span, 3 * width + h * head : 3 * width + (h + 1) * head]
            grad_out = grad_mixed[:, h * head : (h + 1) * head]
            grad_attn = dot(grad_out, values, ((1,), (1,))).astype(bf16)
            grad_scores = (grad_attn.astype(f32) * attn_slope[h]).astype(bf16)
            at = width + h * head
            back[:, at : at + head] = dot(attn[h], grad_out, ((0,), (0,))).astype(bf16)
            at = 2 * width + h * head
            back[:, at : at + head] = dot(grad_scores, keys).astype(bf16)
            at = 3 * width + h * head
            back[:, at : at + head] = dot(grad_scores, queries, ((0,), (0,))).astype(bf16)
        grad_normed = jnp.zeros((slots, columns), f32)
        for i in range(8):
            side = slice(256 * i, 256 * i + 256)
            grad_flat = (dot(collect[m], back[:, side]) * slope[part, side]).astype(bf16)
            grad_normed = grad_normed + dot(grad_flat, weight(i), ((1,), (1,)))
        grad_normed = grad_normed.astype(bf16).astype(f32)
        slot_grad = normalise_back(grad_normed, normed[part], factor[part]).astype(bf16)
        grads[:, m] = slot_grad.reshape(SHARDS, CAP, columns)
        for piece in ((0,), (1, 2))[m]:
            for k in across_table:
                start(slot_send(piece, table_peer(k), shard, k, table_peer(k)))
    arrived[shard] = grads[shard]

    asks = [slot_rows(held, group) for group in range(2)]
    side = columns // 2
    tiles = nz // 2
    lines = blocks // 2

    def half_sums(h):
        for piece in ((0, 1), (2,))[h]:
            for k in reversed(across_table):
                p = table_peer(k)
                slot_send(piece, p, p, k, p).wait_recv()
        dense = jnp.zeros((128, side), f32)
        for group in range(2):
            came = arrived[4 * group : 4 * group + 4, :, :, h * side : (h + 1) * side]
            dense = dense + dot(asks[group], came.reshape(128, side))
        dense = dense.astype(bf16)
        for part in range(NY):
            for r in range(2):
                for b in range(lines):
                    at = part * 32 + r * 16
                    y_send[part, h * tiles + r * lines + b] = dense[
                        at : at + 16, b * 128 : b * 128 + 128
                    ]

    def half_y(h, q, to, k):
        part = pl.ds(h * tiles, tiles)
        return remote(
            y_send.at[q, part], y_got.at[to, part], ry_s.at[h, k], ry_r.at[h, to], along_y(k)
        )

    def half_z(h, j):
        q = lax.rem(z + j, tiles) + h * tiles
        return remote(z_send.at[q], z_got.at[z], rz_s.at[h, j], rz_r.at[z], (q * NY + y, shard))

    around = [tiles // 2]
    for j in range(tiles // 2 - 1, 0, -1):
        around += [j, tiles - j]

    for h in range(2):
        half_sums(h)
        for k in across_y:
            start(half_y(h, y_peer(k), y, k))
    for h in range(2):
        part = slice(h * tiles, (h + 1) * tiles)
        y_sum = y_send[y, part].astype(f32)
        for k in reversed(across_y):
            q = y_peer(k)
            half_y(h, q, q, k).wait_recv()
            y_sum = y_sum + y_got[q, part].astype(f32)
        z_send[part] = y_sum.astype(bf16)
        for j in around:
            start(half_z(h, j))

        @pl.when(z // tiles != h)
        def _():
            half_z(h, 0).start()

    z_sum = z_send[z].astype(f32)
    for k in reversed(across_z):
        q = z_peer(k)
        remote(z_send.at[q], z_got.at[q], rz_s.at[0, 0], rz_r.at[q], (q * NY + y, shard)).wait_recv()
        z_sum = z_sum + z_got[q].astype(f32)
    total[y, z] = z_sum.astype(bf16)

    for k in across_z:
        q = z_peer(k)
        block = total.at[y, z]
        start(remote(block, block, gz_s.at[k], gz_r.at[z], (q * NY + y, shard)))
    def tile_of(q):
        block = total.at[y, q]
        return remote(block, block, gz_s.at[1], gz_r.at[q], (q * NY + y, shard))

    def out_y(h, q, k):
        block = total.at[q, pl.ds(h * tiles, tiles)]
        return remote(block, block, gy_s.at[h, k], gy_r.at[h, q], along_y(k))

    for h in range(2):
        for j in reversed(around):
            tile_of(lax.rem(z + j, tiles) + h * tiles).wait_recv()

        @pl.when(z // tiles != h)
        def _():
            tile_of(lax.rem(z, tiles) + h * tiles).wait_recv()

        for k in across_y:
            start(out_y(h, y, k))

    for k in reversed(across_table):
        p = table_peer(k)
        remote(mom_send.at[p], mom_got.at[p], m_s.at[k], m_r.at[p], (dp, p)).wait_recv()
    def rep_out(h, src, to, k, p):
        return remote(
            rep_send.at[h, src], rep_got.at[h, to], r_s.at[h, k], r_r.at[h, to], (dp, p)
        )

    for h in range(2):
        for k in reversed(across_y):
            out_y(h, y_peer(k), k).wait_recv()
        grad = [
            jnp.concatenate(
                [total[n // 2, h * tiles + (n % 2) * lines + b] for b in range(lines)], axis=1
            ).astype(f32)
            for n in range(8)
        ]
        for p in range(SHARDS):
            own = grad[4 + p // 2][(p % 2) * 8 : (p % 2) * 8 + 8]
            rep_send[h, p] = jnp.concatenate(
                [own[:, : side // 2], own[:, side // 2 :]], axis=0
            ).astype(bf16)
        for k in across_table:
            p = table_peer(k)
            start(rep_out(h, p, shard, k, p))
        rep_got[h, shard] = rep_send[h, shard]
        over = slice(h * side, (h + 1) * side)
        for n in range(8):
            span = slice(16 * n, 16 * n + 16)
            first_out[span, over] = beta_one * first_ref[span, over] + (1.0 - beta_one) * grad[n]
            second_out[span, over] = beta_two * second_ref[span, over] + (1.0 - beta_two) * (
                grad[n] * grad[n]
            )
    for h in range(2):
        over = slice(h * side, (h + 1) * side)
        for k in reversed(across_table):
            p = table_peer(k)
            rep_out(h, p, p, k, p).wait_recv()
        rep_first, rep_second = [], []
        for p in range(SHARDS):
            halves = rep_got[h, p].astype(f32)
            grad = jnp.concatenate([halves[:8], halves[8:]], axis=1)
            moments = mom_got[p, :, over].astype(f32)
            rep_first.append(beta_one * moments[:8] + (1.0 - beta_one) * grad)
            rep_second.append(beta_two * moments[8:] + (1.0 - beta_two) * (grad * grad))
        rep_first = dot(pick, jnp.concatenate(rep_first, axis=0).astype(bf16))
        rep_second = dot(pick, jnp.concatenate(rep_second, axis=0).astype(bf16))
        first_out[:, over] = (first_out[:, over] + rep_first) * scale
        second_out[:, over] = (second_out[:, over] + rep_second) * scale
    for h in range(2):

        @pl.when(z // tiles != h)
        def _():
            half_z(h, 0).wait_send()

    for copy in started:
        copy.wait_send()


def body(
    nz,
    token_slot,
    seg_ids,
    req_rows,
    cotangent,
    uvqk_weight,
    table,
    first_moment,
    second_moment,
    dup_count,
    dup_target,
):
    columns = table.shape[1]
    count = token_slot.shape[2]
    tokens = MICRO * count
    slots = SHARDS * CAP
    vmem = pl.BlockSpec(memory_space=pltpu.VMEM)
    hbm = pl.BlockSpec(memory_space=pl.ANY)
    dma = pltpu.SemaphoreType.DMA
    bf16, f32, i32 = jnp.bfloat16, jnp.float32, jnp.int32

    tiles = 2 * columns // 128
    first, second = pl.pallas_call(
        functools.partial(whole_kernel, nz),
        out_shape=(
            jax.ShapeDtypeStruct(table.shape, f32),
            jax.ShapeDtypeStruct(table.shape, f32),
        ),
        in_specs=[hbm] * 10,
        out_specs=(vmem,) * 2,
        scratch_shapes=[
            pltpu.VMEM(req_rows.shape, i32),
            pltpu.VMEM(token_slot.shape, i32),
            pltpu.VMEM(seg_ids.shape, i32),
            pltpu.VMEM((1, SHARDS * SHARDS), i32),
            pltpu.VMEM((DCAP, SHARDS * SHARDS), i32),
            pltpu.VMEM((SHARDS, 8, 128), i32),
            pltpu.VMEM((SHARDS, 8, 128), i32),
            pltpu.VMEM(table.shape, bf16),
            pltpu.VMEM((NX, 2, 2, nz, NY, 16, 128), bf16),
            pltpu.VMEM((MICRO, count, 512), bf16),
            pltpu.VMEM(table.shape, f32),
            pltpu.VMEM(table.shape, f32),
            pltpu.VMEM((SHARDS, MICRO, CAP, columns), bf16),
            pltpu.VMEM((SHARDS, MICRO, CAP, columns), bf16),
            pltpu.VMEM((MICRO * slots, 2048), f32),
            pltpu.VMEM((tokens, 2048), bf16),
            pltpu.VMEM((HEADS, count, count), bf16),
            pltpu.VMEM((HEADS, count, count), f32),
            pltpu.VMEM((count, 512), f32),
            pltpu.VMEM((count, 2048), bf16),
            pltpu.VMEM((SHARDS, MICRO, CAP, columns), bf16),
            pltpu.VMEM((SHARDS, MICRO, CAP, columns), bf16),
            pltpu.VMEM((NY, tiles, 16, 128), bf16),
            pltpu.VMEM((NY, tiles, 16, 128), bf16),
            pltpu.VMEM((tiles, 16, 128), bf16),
            pltpu.VMEM((tiles, 16, 128), bf16),
            pltpu.VMEM((NY, tiles, 16, 128), bf16),
            pltpu.VMEM((SHARDS, 16, columns), bf16),
            pltpu.VMEM((SHARDS, 16, columns), bf16),
            pltpu.VMEM((2, SHARDS, 16, columns // 4), bf16),
            pltpu.VMEM((2, SHARDS, 16, columns // 4), bf16),
            dma((11,)),
            dma((SHARDS,)),
            dma((SHARDS,)),
            dma((SHARDS,)),
            dma((SHARDS,)),
            dma((nz,)),
            dma((nz,)),
            dma((4, 4)),
            dma((4, 4)),
            dma((8,)),
            dma((8,)),
            dma((3, SHARDS)),
            dma((3, SHARDS)),
            dma((2, NY)),
            dma((2, NY)),
            dma((2, nz // 2)),
            dma((nz,)),
            dma((nz,)),
            dma((nz,)),
            dma((2, NY)),
            dma((2, NY)),
            dma((SHARDS,)),
            dma((SHARDS,)),
            dma((2, SHARDS)),
            dma((2, SHARDS)),
        ],
        compiler_params=pltpu.CompilerParams(
            collective_id=0, has_side_effects=True, vmem_limit_bytes=63 << 20
        ),
        name="whole",
    )(
        req_rows,
        token_slot,
        seg_ids,
        dup_count[None, :],
        dup_target.T,
        table,
        uvqk_weight,
        cotangent,
        first_moment,
        second_moment,
    )
    keep = second > 0.0
    new_first = jnp.where(keep, first, 0.0)
    new_second = jnp.where(keep, second, 0.0)
    update = table.astype(f32) - learn_rate * new_first / (jnp.sqrt(new_second) + adam_eps)
    return (jnp.where(keep, update, 0.0).astype(bf16), new_first, new_second)


def solution(mesh):
    placed = (
        P(None, ("dp", "table"), None),
        P(None, ("dp", "table"), None),
        P(None, ("dp", "table"), None),
        P(None, ("dp", "table"), None),
        P("dp", None),
        P("table", None),
        P("table", None),
        P("table", None),
        P(),
        P(),
    )
    return jax.shard_map(
        functools.partial(body, mesh.shape["dp"] // NY),
        mesh=mesh,
        in_specs=placed,
        out_specs=(P("table", None), P("table", None), P("table", None)),
        check_vma=False,
    )
```

```python
import functools

import jax
import jax.numpy as jnp
from jax import lax
from jax.experimental import pallas as pl
from jax.experimental.pallas import tpu as pltpu
from jax.sharding import PartitionSpec as P

MESH = pl.DeviceIdType.MESH
HEADS = 4
MICRO = 2
NX = 4
NY = 4
SHARDS = 8
CAP = 16
DCAP = 8

beta_one = 0.9
beta_two = 0.999
learn_rate = 0.1
adam_eps = 1e-08
norm_eps = 1e-05


def dot(a, b, dims=((1,), (0,))):
    return lax.dot_general(a, b, (dims, ((), ())), preferred_element_type=jnp.float32)


def place():
    dp = lax.axis_index("dp")
    shard = lax.axis_index("table")
    return dp // NY, dp % NY, shard // 2, shard % 2, dp, shard


def greet(peers):
    barrier = pltpu.get_barrier_semaphore()
    for peer in peers:
        pl.semaphore_signal(barrier, inc=1, device_id=peer, device_id_type=MESH)
    pl.semaphore_wait(barrier, len(peers))


def remote(src, dst, send, recv, peer):
    return pltpu.make_async_remote_copy(
        src_ref=src, dst_ref=dst, send_sem=send, recv_sem=recv, device_id=peer, device_id_type=MESH
    )


def slot_rows(held_ref, group):
    rows = held_ref[4 * group]
    for peer in range(1, 4):
        rows = jnp.maximum(rows, held_ref[4 * group + peer])
    number = lax.broadcasted_iota(jnp.int32, (128, 128), 0)
    return jnp.where(number == rows[0:1], 1.0, 0.0).astype(jnp.bfloat16)


def normalise(values):
    center = jnp.mean(values, axis=-1, keepdims=True)
    shifted = values - center
    spread = jnp.mean(shifted * shifted, axis=-1, keepdims=True)
    factor = lax.rsqrt(spread + norm_eps)
    return shifted * factor, factor


def normalise_back(grad, normed, factor):
    grad_mean = jnp.mean(grad, axis=-1, keepdims=True)
    along = jnp.mean(grad * normed, axis=-1, keepdims=True)
    return factor * (grad - grad_mean - normed * along)


def sigmoid(values):
    return 0.5 * jnp.tanh(0.5 * values) + 0.5


def whole_kernel(
    nz,
    req_hbm,
    slot_hbm,
    seg_hbm,
    tally_hbm,
    target_hbm,
    table_hbm,
    w_hbm,
    cot_hbm,
    first_hbm,
    second_hbm,
    first_out,
    second_out,
    req_ref,
    slot_ref,
    seg_ref,
    tally_ref,
    target_ref,
    asked,
    held,
    table_ref,
    wout,
    cot_ref,
    first_ref,
    second_ref,
    found,
    fetched,
    slope,
    flow,
    attn,
    attn_slope,
    mixed,
    back,
    grads,
    arrived,
    y_send,
    y_got,
    z_send,
    z_got,
    far,
    total,
    mom_send,
    mom_got,
    rep_send,
    rep_got,
    local_s,
    req_s,
    req_r,
    fnd_s,
    fnd_r,
    z_s,
    z_r,
    ring_s,
    ring_r,
    core_s,
    core_r,
    a_s,
    a_r,
    ry_s,
    ry_r,
    rz_s,
    rz_r,
    fz_s,
    fz_r,
    gz_s,
    gz_r,
    gy_s,
    gy_r,
    m_s,
    m_r,
    r_s,
    r_r,
):
    z, y, x, core, dp, shard = place()
    other = 1 - core
    half = nz // 2
    columns = table_ref.shape[1]
    blocks = columns // 128
    f32, bf16 = jnp.float32, jnp.bfloat16

    def table_peer(k):
        return lax.rem(shard + k, SHARDS)

    def z_peer(k):
        return lax.rem(z + k, nz)

    def y_peer(k):
        return lax.rem(y + k, NY)

    def along_y(k):
        return (z * NY + y_peer(k), shard)

    def along_x(k):
        return (dp, lax.rem(x + k, NX) * 2 + core)

    across_table = (4, 3, 5, 2, 6, 1, 7)
    across_z = [nz // 2]
    for k in range(nz // 2 - 1, 0, -1):
        across_z += [k, nz - k]
    across_y = (2, 1, 3)

    local = [(req_hbm, req_ref)]
    for g in range(2):
        part = pl.ds(pl.multiple_of(shard * 256 + g * 128, 128), 128)
        local.append((w_hbm.at[:, part], wout.at[x, core, g, z, y]))
    local += [
        (table_hbm, table_ref),
        (cot_hbm, cot_ref),
        (first_hbm, first_ref),
        (second_hbm, second_ref),
        (slot_hbm, slot_ref),
        (seg_hbm, seg_ref),
        (tally_hbm, tally_ref),
        (target_hbm, target_ref),
    ]
    local = [pltpu.make_async_copy(a, b, local_s.at[i]) for i, (a, b) in enumerate(local)]
    for copy in local:
        copy.start()

    local[0].wait()
    lane = lax.broadcasted_iota(jnp.int32, (CAP, 128), 1) % 32
    deep = lax.broadcasted_iota(jnp.int32, (CAP, 128), 0)
    wide = jnp.zeros((SHARDS, 128), f32)
    for m in range(MICRO):
        spot = jnp.where(lane == deep + m * CAP, 1.0, 0.0).astype(bf16)
        wide = wide + dot(req_ref[m].astype(f32).astype(bf16), spot)
    mine = lax.broadcasted_iota(jnp.int32, (SHARDS, 128), 1) // 32 == lax.rem(shard, 4)
    wide = jnp.where(mine, wide.astype(jnp.int32), -1)
    for p in range(SHARDS):
        asked[p] = jnp.broadcast_to(wide[p : p + 1], (8, 128))

    greet(
        [(dp, table_peer(k)) for k in range(1, SHARDS)]
        + [(z_peer(k) * NY + y, shard) for k in range(1, nz)]
        + [along_y(k) for k in range(1, NY)]
    )

    started = []

    def start(copy):
        copy.start()
        started.append(copy)
        return copy

    def drain():
        for copy in started:
            copy.wait_send()
        started.clear()

    local[1].wait()
    local[2].wait()
    for k in across_z:
        q = z_peer(k)
        block = wout.at[x, core, :, z, y]
        start(remote(block, block, z_s.at[k], z_r.at[z], (q * NY + y, shard)))

    for k in across_table:
        p = table_peer(k)
        start(remote(asked.at[p], held.at[shard], req_s.at[k], req_r.at[shard], (dp, p)))
    held[shard] = asked[shard]

    local[3].wait()
    for k in reversed(across_table):
        p = table_peer(k)
        remote(asked.at[p], held.at[p], req_s.at[k], req_r.at[p], (dp, p)).wait_recv()
    for group in range(2):
        rows = dot(slot_rows(held, group), table_ref[...], ((0,), (0,)))
        found[4 * group : 4 * group + 4] = rows.astype(bf16).reshape(4, MICRO, CAP, columns)
    for k in across_table:
        p = table_peer(k)
        start(remote(found.at[p], fetched.at[shard], fnd_s.at[k], fnd_r.at[shard], (dp, p)))
    fetched[shard] = found[shard]

    for k in reversed(across_z):
        q = z_peer(k)
        block = wout.at[x, core, :, q, y]
        remote(block, block, z_s.at[k], z_r.at[q], (q * NY + y, shard)).wait_recv()

    whole, low, high = pl.ds(0, nz), pl.ds(0, half), pl.ds(half, half)
    views = (
        lambda i, zs: wout.at[x, core, 0, zs, i],
        lambda i, zs: wout.at[i, core, 1, zs, y],
        lambda i, zs: wout.at[i, core, 0, zs],
        lambda i, zs: wout.at[:, core, 1, zs, i],
    )
    spots = (y, x, x, y)
    steps = (along_y, along_x, along_x, along_y)

    def link(ring, which, offset, zs, to):
        block = views[ring](lax.rem(spots[ring] + offset, 4), zs)
        return remote(
            block, block, ring_s.at[ring, which], ring_r.at[ring, which], steps[ring](to)
        )

    def ring_first(ring):
        start(link(ring, 0, 0, whole, 1))
        start(link(ring, 1, 0, whole, 3))

    def ring_second(ring):
        link(ring, 0, 3, whole, 1).wait_recv()
        start(link(ring, 2, 3, low, 1))
        link(ring, 1, 1, whole, 3).wait_recv()
        start(link(ring, 3, 1, high, 3))

    def ring_third(ring):
        link(ring, 2, 2, low, 1).wait_recv()
        link(ring, 3, 2, high, 3).wait_recv()

    def across(ring, offset, mine=True):
        i = lax.rem(spots[ring] + offset, 4)
        c = core if mine else other
        block = wout.at[i, c, 0] if ring == 2 else wout.at[:, c, 1, :, i]
        s = (ring - 2) * 4 + offset
        return remote(block, block, core_s.at[s], core_r.at[s], (dp, x * 2 + other))

    for ring in (0, 1):
        ring_first(ring)
    for ring in (0, 1):
        ring_second(ring)
    for ring in (0, 1):
        ring_third(ring)
    for ring in (2, 3):
        ring_first(ring)
        start(across(ring, 0))

    for k in reversed(across_table):
        p = table_peer(k)
        remote(found.at[p], fetched.at[p], fnd_s.at[k], fnd_r.at[p], (dp, p)).wait_recv()
    for copy in local[7:]:
        copy.wait()
    count = seg_ref.shape[2]
    slots = SHARDS * CAP
    collect, expand, share = [], [], []
    number = lax.broadcasted_iota(jnp.int32, (slots, count), 0)
    user = lax.broadcasted_iota(jnp.int32, (8, count), 0)
    causal = lax.broadcasted_iota(jnp.int32, (count, count), 0) >= lax.broadcasted_iota(
        jnp.int32, (count, count), 1
    )
    for m in range(MICRO):
        hot = jnp.where(number == slot_ref[m], 1.0, 0.0)
        collect.append(hot.astype(bf16))
        expand.append(jnp.transpose(hot).astype(bf16))
        belongs = jnp.where(user == seg_ref[m], 1.0, 0.0).astype(bf16)
        same = dot(belongs, belongs, ((0,), (0,)))
        history = jnp.sum(same, axis=1, keepdims=True)
        share.append(jnp.where(causal, same, 0.0) / history)
    rows = jnp.concatenate(
        [fetched[:, m].reshape(slots, columns) for m in range(MICRO)], axis=0
    ).astype(f32)
    normed, factor = normalise(rows)
    given = normed.astype(bf16)

    i32 = jnp.int32
    live = lax.broadcasted_iota(i32, (DCAP, 64), 0) < tally_ref[...]
    aims = jnp.where(live, target_ref[...] + 1, 0).astype(f32).astype(bf16)
    lane = lax.broadcasted_iota(i32, (64, 64), 1)
    deep = lax.broadcasted_iota(i32, (64, 64), 0)
    here = jnp.where(deep == (lane // DCAP) * SHARDS + shard, 1.0, 0.0).astype(bf16)
    aims = dot(aims, here)
    lane = lax.broadcasted_iota(i32, (DCAP, 64), 1) % DCAP
    deep = lax.broadcasted_iota(i32, (DCAP, 64), 0)
    aims = jnp.sum(jnp.where(lane == deep, aims, 0.0), axis=0, keepdims=True).astype(i32) - 1
    number = lax.broadcasted_iota(i32, (128, 64), 0)
    pick = jnp.where(number == aims, 1.0, 0.0)
    tally = jnp.sum(pick, axis=1, keepdims=True)
    pick = pick.astype(bf16)
    lane = lax.broadcasted_iota(i32, (64, 64), 1)
    deep = lax.broadcasted_iota(i32, (64, 64), 0)
    limit = jnp.where(lane == shard * SHARDS + deep // DCAP, tally_ref[...].astype(f32), 0.0)
    limit = jnp.sum(limit, axis=1, keepdims=True)
    row = (lax.broadcasted_iota(i32, (64, 1), 0) % DCAP).astype(f32)
    scale = 1.0 / (1.0 + tally)
    scale = jnp.concatenate([scale[:64], jnp.where(row < limit, 0.0, scale[64:])], axis=0)

    for ring in (2, 3):
        ring_second(ring)
        start(across(ring, 3))
        start(across(ring, 1))
    for ring in (2, 3):
        ring_third(ring)
        start(across(ring, 2))

    for copy in local[4:7]:
        copy.wait()
    for p in range(SHARDS):
        line = slice(64 + DCAP * p, 64 + DCAP * p + DCAP)
        mom_send[p] = jnp.concatenate([first_ref[line], second_ref[line]], axis=0).astype(bf16)
    for ring in (2, 3):
        for offset in (0, 3, 1, 2):
            across(ring, offset, mine=False).wait_recv()
    for k in across_table:
        p = table_peer(k)
        start(remote(mom_send.at[p], mom_got.at[shard], m_s.at[k], m_r.at[shard], (dp, p)))
    mom_got[shard] = mom_send[shard]

    width = 512
    head = width // HEADS

    def weight(i):
        sides = [wout[i // 2, i % 2, g].reshape(columns, 128) for g in range(2)]
        return jnp.concatenate(sides, axis=1)

    for i in range(8):
        flat = dot(given, weight(i))
        sig = sigmoid(flat)
        value = flat * sig
        slope[:, 256 * i : 256 * i + 256] = sig * (1.0 + flat * (1.0 - sig))
        top = value.astype(bf16)
        for m in range(MICRO):
            span = slice(m * count, (m + 1) * count)
            part = slice(m * slots, (m + 1) * slots)
            spread = dot(expand[m], top[part])
            flow[span, 256 * i : 256 * i + 256] = spread.astype(bf16)

    def slot_send(m, src, to, k, p):
        return remote(
            grads.at[src, m], arrived.at[to, m], a_s.at[m, k], a_r.at[m, to], (dp, p)
        )

    factor_scale = head ** (-0.5)
    for m in range(MICRO):
        span = slice(m * count, (m + 1) * count)
        part = slice(m * slots, (m + 1) * slots)
        for h in range(HEADS):
            values = flow[span, width + h * head : width + (h + 1) * head]
            queries = flow[span, 2 * width + h * head : 2 * width + (h + 1) * head]
            keys = flow[span, 3 * width + h * head : 3 * width + (h + 1) * head]
            scores = dot(queries, keys, ((1,), (1,))) * factor_scale
            sig = sigmoid(scores)
            shared = share[m] * sig
            weights = (scores * shared).astype(bf16)
            attn[h] = weights
            attn_slope[h] = shared * (1.0 + scores * (1.0 - sig)) * factor_scale
            mixed[:, h * head : (h + 1) * head] = dot(weights, values)
        level, spread = normalise(mixed[...])
        upstream = cot_ref[m].astype(f32)
        back[:, :width] = (upstream * level).astype(bf16)
        grad_mixed = normalise_back(
            upstream * flow[span, :width].astype(f32), level, spread
        ).astype(bf16)
        for h in range(HEADS):
            values = flow[span, width + h * head : width + (h + 1) * head]
            queries = flow[span, 2 * width + h * head : 2 * width + (h + 1) * head]
            keys = flow[span, 3 * width + h * head : 3 * width + (h + 1) * head]
            grad_out = grad_mixed[:, h * head : (h + 1) * head]
            grad_attn = dot(grad_out, values, ((1,), (1,))).astype(bf16)
            grad_scores = (grad_attn.astype(f32) * attn_slope[h]).astype(bf16)
            at = width + h * head
            back[:, at : at + head] = dot(attn[h], grad_out, ((0,), (0,))).astype(bf16)
            at = 2 * width + h * head
            back[:, at : at + head] = dot(grad_scores, keys).astype(bf16)
            at = 3 * width + h * head
            back[:, at : at + head] = dot(grad_scores, queries, ((0,), (0,))).astype(bf16)
        grad_normed = jnp.zeros((slots, columns), f32)
        for i in range(8):
            side = slice(256 * i, 256 * i + 256)
            grad_flat = (dot(collect[m], back[:, side]) * slope[part, side]).astype(bf16)
            grad_normed = grad_normed + dot(grad_flat, weight(i), ((1,), (1,)))
        grad_normed = grad_normed.astype(bf16).astype(f32)
        slot_grad = normalise_back(grad_normed, normed[part], factor[part]).astype(bf16)
        grads[:, m] = slot_grad.reshape(SHARDS, CAP, columns)
        for k in across_table:
            start(slot_send(m, table_peer(k), shard, k, table_peer(k)))
    arrived[shard] = grads[shard]

    asks = [slot_rows(held, group) for group in range(2)]
    for m in range(MICRO):
        for k in reversed(across_table):
            p = table_peer(k)
            slot_send(m, p, p, k, p).wait_recv()
    dense = jnp.zeros((128, columns), f32)
    for group in range(2):
        came = arrived[4 * group : 4 * group + 4].reshape(128, columns)
        dense = dense + dot(asks[group], came)
    dense = dense.astype(bf16)
    for part in range(NY):
        for r in range(2):
            for b in range(blocks):
                at = part * 32 + r * 16
                y_send[part, r * blocks + b] = dense[at : at + 16, b * 128 : b * 128 + 128]

    def sum_y(q, to, k):
        return remote(y_send.at[q], y_got.at[to], ry_s.at[k], ry_r.at[to], along_y(k))

    for k in across_y:
        start(sum_y(y_peer(k), y, k))
    drain()
    y_sum = y_send[y].astype(f32)
    for k in reversed(across_y):
        sum_y(y_peer(k), y_peer(k), k).wait_recv()
        y_sum = y_sum + y_got[y_peer(k)].astype(f32)
    z_send[...] = y_sum.astype(bf16)

    quarter = 2 * blocks // 4
    rank, near, laps = z % 4, z // 4, nz // 4

    def own(i):
        return pl.ds(i * quarter, quarter)

    def sum_near(q, to, k):
        peer = (near * 4 + lax.rem(rank + k, 4)) * NY + y
        return remote(z_send.at[own(q)], z_got.at[to], rz_s.at[k], rz_r.at[to], (peer, shard))

    def sum_far(to, k):
        peer = (lax.rem(near + k, laps) * 4 + rank) * NY + y
        return remote(far.at[near], far.at[to], fz_s.at[k], fz_r.at[to], (peer, shard))

    for k in (2, 1, 3):
        start(sum_near(lax.rem(rank + k, 4), rank, k))
    z_sum = z_send[own(rank)].astype(f32)
    for k in (1, 3, 2):
        q = lax.rem(rank + k, 4)
        sum_near(q, q, k).wait_recv()
        z_sum = z_sum + z_got[q].astype(f32)
    far[near] = z_sum.astype(bf16)
    for k in range(laps - 1, 0, -1):
        start(sum_far(near, k))
    for k in range(1, laps):
        sum_far(lax.rem(near + k, laps), k).wait_recv()
    z_sum = far[0].astype(f32)
    for i in range(1, laps):
        z_sum = z_sum + far[i].astype(f32)
    total[y, own(rank)] = z_sum.astype(bf16)

    def out_z(q, k):
        block = total.at[y, own(q)]
        peer = z_peer((0, 1, 2, nz - 1)[k]) * NY + y
        return remote(block, block, gz_s.at[k], gz_r.at[q], (peer, shard))

    for k in (2, 1, 3):
        start(out_z(rank, k))
    for k in (1, 3, 2):
        q = lax.rem(rank + k, 4)
        out_z(q, k).wait_recv()

    def out_y(q, k):
        return remote(total.at[q], total.at[q], gy_s.at[k], gy_r.at[q], along_y(k))

    for k in across_y:
        start(out_y(y, k))
    for k in reversed(across_table):
        p = table_peer(k)
        remote(mom_send.at[p], mom_got.at[p], m_s.at[k], m_r.at[p], (dp, p)).wait_recv()
    def rep_out(src, to, k, p):
        return remote(rep_send.at[src], rep_got.at[to], r_s.at[k], r_r.at[to], (dp, p))

    for k in reversed(across_y):
        out_y(y_peer(k), k).wait_recv()
    grad = [
        jnp.concatenate(
            [total[n // 2, (n % 2) * blocks + b] for b in range(blocks)], axis=1
        ).astype(f32)
        for n in range(8)
    ]
    for p in range(SHARDS):
        sent = grad[4 + p // 2][(p % 2) * 8 : (p % 2) * 8 + 8]
        rep_send[p] = jnp.concatenate(
            [sent[:, : columns // 2], sent[:, columns // 2 :]], axis=0
        ).astype(bf16)
    for k in across_table:
        p = table_peer(k)
        start(rep_out(p, shard, k, p))
    rep_got[shard] = rep_send[shard]
    for n in range(8):
        span = slice(16 * n, 16 * n + 16)
        first_out[span] = beta_one * first_ref[span] + (1.0 - beta_one) * grad[n]
        second_out[span] = beta_two * second_ref[span] + (1.0 - beta_two) * (grad[n] * grad[n])
    drain()
    for k in reversed(across_table):
        p = table_peer(k)
        rep_out(p, p, k, p).wait_recv()
    rep_first, rep_second = [], []
    for p in range(SHARDS):
        halves = rep_got[p].astype(f32)
        grad = jnp.concatenate([halves[:8], halves[8:]], axis=1)
        moments = mom_got[p].astype(f32)
        rep_first.append(beta_one * moments[:8] + (1.0 - beta_one) * grad)
        rep_second.append(beta_two * moments[8:] + (1.0 - beta_two) * (grad * grad))
    rep_first = dot(pick, jnp.concatenate(rep_first, axis=0).astype(bf16))
    rep_second = dot(pick, jnp.concatenate(rep_second, axis=0).astype(bf16))
    first_out[...] = (first_out[...] + rep_first) * scale
    second_out[...] = (second_out[...] + rep_second) * scale


def body(
    nz,
    token_slot,
    seg_ids,
    req_rows,
    cotangent,
    uvqk_weight,
    table,
    first_moment,
    second_moment,
    dup_count,
    dup_target,
):
    columns = table.shape[1]
    count = token_slot.shape[2]
    tokens = MICRO * count
    slots = SHARDS * CAP
    vmem = pl.BlockSpec(memory_space=pltpu.VMEM)
    hbm = pl.BlockSpec(memory_space=pl.ANY)
    dma = pltpu.SemaphoreType.DMA
    bf16, f32, i32 = jnp.bfloat16, jnp.float32, jnp.int32

    tiles = 2 * columns // 128
    first, second = pl.pallas_call(
        functools.partial(whole_kernel, nz),
        out_shape=(
            jax.ShapeDtypeStruct(table.shape, f32),
            jax.ShapeDtypeStruct(table.shape, f32),
        ),
        in_specs=[hbm] * 10,
        out_specs=(vmem,) * 2,
        scratch_shapes=[
            pltpu.VMEM(req_rows.shape, i32),
            pltpu.VMEM(token_slot.shape, i32),
            pltpu.VMEM(seg_ids.shape, i32),
            pltpu.VMEM((1, SHARDS * SHARDS), i32),
            pltpu.VMEM((DCAP, SHARDS * SHARDS), i32),
            pltpu.VMEM((SHARDS, 8, 128), i32),
            pltpu.VMEM((SHARDS, 8, 128), i32),
            pltpu.VMEM(table.shape, bf16),
            pltpu.VMEM((NX, 2, 2, nz, NY, 16, 128), bf16),
            pltpu.VMEM((MICRO, count, 512), bf16),
            pltpu.VMEM(table.shape, f32),
            pltpu.VMEM(table.shape, f32),
            pltpu.VMEM((SHARDS, MICRO, CAP, columns), bf16),
            pltpu.VMEM((SHARDS, MICRO, CAP, columns), bf16),
            pltpu.VMEM((MICRO * slots, 2048), f32),
            pltpu.VMEM((tokens, 2048), bf16),
            pltpu.VMEM((HEADS, count, count), bf16),
            pltpu.VMEM((HEADS, count, count), f32),
            pltpu.VMEM((count, 512), f32),
            pltpu.VMEM((count, 2048), bf16),
            pltpu.VMEM((SHARDS, MICRO, CAP, columns), bf16),
            pltpu.VMEM((SHARDS, MICRO, CAP, columns), bf16),
            pltpu.VMEM((NY, tiles, 16, 128), bf16),
            pltpu.VMEM((NY, tiles, 16, 128), bf16),
            pltpu.VMEM((tiles, 16, 128), bf16),
            pltpu.VMEM((4, tiles // 4, 16, 128), bf16),
            pltpu.VMEM((nz // 4, tiles // 4, 16, 128), bf16),
            pltpu.VMEM((NY, tiles, 16, 128), bf16),
            pltpu.VMEM((SHARDS, 16, columns), bf16),
            pltpu.VMEM((SHARDS, 16, columns), bf16),
            pltpu.VMEM((SHARDS, 16, columns // 2), bf16),
            pltpu.VMEM((SHARDS, 16, columns // 2), bf16),
            dma((11,)),
            dma((SHARDS,)),
            dma((SHARDS,)),
            dma((SHARDS,)),
            dma((SHARDS,)),
            dma((nz,)),
            dma((nz,)),
            dma((4, 4)),
            dma((4, 4)),
            dma((8,)),
            dma((8,)),
            dma((MICRO, SHARDS)),
            dma((MICRO, SHARDS)),
            dma((NY,)),
            dma((NY,)),
            dma((4,)),
            dma((4,)),
            dma((nz // 4,)),
            dma((nz // 4,)),
            dma((4,)),
            dma((4,)),
            dma((NY,)),
            dma((NY,)),
            dma((SHARDS,)),
            dma((SHARDS,)),
            dma((SHARDS,)),
            dma((SHARDS,)),
        ],
        compiler_params=pltpu.CompilerParams(
            collective_id=0, has_side_effects=True, vmem_limit_bytes=63 << 20
        ),
        name="whole",
    )(
        req_rows,
        token_slot,
        seg_ids,
        dup_count[None, :],
        dup_target.T,
        table,
        uvqk_weight,
        cotangent,
        first_moment,
        second_moment,
    )
    keep = second > 0.0
    new_first = jnp.where(keep, first, 0.0)
    new_second = jnp.where(keep, second, 0.0)
    update = table.astype(f32) - learn_rate * new_first / (jnp.sqrt(new_second) + adam_eps)
    return (jnp.where(keep, update, 0.0).astype(bf16), new_first, new_second)


def solution(mesh):
    placed = (
        P(None, ("dp", "table"), None),
        P(None, ("dp", "table"), None),
        P(None, ("dp", "table"), None),
        P(None, ("dp", "table"), None),
        P("dp", None),
        P("table", None),
        P("table", None),
        P("table", None),
        P(),
        P(),
    )
    return jax.shard_map(
        functools.partial(body, mesh.shape["dp"] // NY),
        mesh=mesh,
        in_specs=placed,
        out_specs=(P("table", None), P("table", None), P("table", None)),
        check_vma=False,
    )
```

```python
import functools

import jax
import jax.numpy as jnp
from jax import lax
from jax.experimental import pallas as pl
from jax.experimental.pallas import tpu as pltpu
from jax.sharding import PartitionSpec as P

MESH = pl.DeviceIdType.MESH
HEADS = 4
MICRO = 2
NX = 4
NY = 4
SHARDS = 8
CAP = 16
DCAP = 8

beta_one = 0.9
beta_two = 0.999
learn_rate = 0.1
adam_eps = 1e-08
norm_eps = 1e-05


def dot(a, b, dims=((1,), (0,))):
    return lax.dot_general(a, b, (dims, ((), ())), preferred_element_type=jnp.float32)


def place():
    dp = lax.axis_index("dp")
    shard = lax.axis_index("table")
    return dp // NY, dp % NY, shard // 2, shard % 2, dp, shard


def greet(peers):
    barrier = pltpu.get_barrier_semaphore()
    for peer in peers:
        pl.semaphore_signal(barrier, inc=1, device_id=peer, device_id_type=MESH)
    pl.semaphore_wait(barrier, len(peers))


def remote(src, dst, send, recv, peer):
    return pltpu.make_async_remote_copy(
        src_ref=src, dst_ref=dst, send_sem=send, recv_sem=recv, device_id=peer, device_id_type=MESH
    )


def slot_rows(held_ref, group):
    rows = held_ref[4 * group]
    for peer in range(1, 4):
        rows = jnp.maximum(rows, held_ref[4 * group + peer])
    number = lax.broadcasted_iota(jnp.int32, (128, 128), 0)
    return jnp.where(number == rows[0:1], 1.0, 0.0).astype(jnp.bfloat16)


def normalise(values):
    center = jnp.mean(values, axis=-1, keepdims=True)
    shifted = values - center
    spread = jnp.mean(shifted * shifted, axis=-1, keepdims=True)
    factor = lax.rsqrt(spread + norm_eps)
    return shifted * factor, factor


def normalise_back(grad, normed, factor):
    grad_mean = jnp.mean(grad, axis=-1, keepdims=True)
    along = jnp.mean(grad * normed, axis=-1, keepdims=True)
    return factor * (grad - grad_mean - normed * along)


def sigmoid(values):
    return 0.5 * jnp.tanh(0.5 * values) + 0.5


def whole_kernel(
    nz,
    req_hbm,
    slot_hbm,
    seg_hbm,
    tally_hbm,
    target_hbm,
    table_hbm,
    w_hbm,
    cot_hbm,
    first_hbm,
    second_hbm,
    first_out,
    second_out,
    req_ref,
    slot_ref,
    seg_ref,
    tally_ref,
    target_ref,
    asked,
    held,
    table_ref,
    wout,
    cot_ref,
    first_ref,
    second_ref,
    found,
    fetched,
    given_y,
    sums,
    slope,
    flow,
    attn,
    attn_slope,
    mixed,
    back,
    grads,
    arrived,
    y_send,
    y_got,
    z_send,
    z_got,
    total,
    mom_send,
    mom_got,
    rep_send,
    rep_got,
    local_s,
    req_s,
    req_r,
    fnd_s,
    fnd_r,
    z_s,
    z_r,
    ring_s,
    ring_r,
    core_s,
    core_r,
    a_s,
    a_r,
    ry_s,
    ry_r,
    rz_s,
    rz_r,
    gz_s,
    gz_r,
    gy_s,
    gy_r,
    m_s,
    m_r,
    r_s,
    r_r,
):
    z, y, x, core, dp, shard = place()
    other = 1 - core
    half = nz // 2
    columns = table_ref.shape[1]
    blocks = columns // 128
    f32, bf16 = jnp.float32, jnp.bfloat16

    def table_peer(k):
        return lax.rem(shard + k, SHARDS)

    def z_peer(k):
        return lax.rem(z + k, nz)

    def y_peer(k):
        return lax.rem(y + k, NY)

    def along_y(k):
        return (z * NY + y_peer(k), shard)

    def along_x(k):
        return (dp, lax.rem(x + k, NX) * 2 + core)

    across_table = (4, 3, 5, 2, 6, 1, 7)
    across_z = [nz // 2]
    for k in range(nz // 2 - 1, 0, -1):
        across_z += [k, nz - k]
    across_y = (2, 1, 3)

    local = [(req_hbm, req_ref)]
    for g in range(2):
        part = pl.ds(pl.multiple_of(shard * 256 + g * 128, 128), 128)
        local.append((w_hbm.at[:, part], wout.at[x, core, g, z, y]))
    local += [
        (table_hbm, table_ref),
        (cot_hbm, cot_ref),
        (first_hbm, first_ref),
        (second_hbm, second_ref),
        (slot_hbm, slot_ref),
        (seg_hbm, seg_ref),
        (tally_hbm, tally_ref),
        (target_hbm, target_ref),
    ]
    local = [pltpu.make_async_copy(a, b, local_s.at[i]) for i, (a, b) in enumerate(local)]
    for copy in local:
        copy.start()

    local[0].wait()
    lane = lax.broadcasted_iota(jnp.int32, (CAP, 128), 1) % 32
    deep = lax.broadcasted_iota(jnp.int32, (CAP, 128), 0)
    wide = jnp.zeros((SHARDS, 128), f32)
    for m in range(MICRO):
        spot = jnp.where(lane == deep + m * CAP, 1.0, 0.0).astype(bf16)
        wide = wide + dot(req_ref[m].astype(f32).astype(bf16), spot)
    mine = lax.broadcasted_iota(jnp.int32, (SHARDS, 128), 1) // 32 == lax.rem(shard, 4)
    wide = jnp.where(mine, wide.astype(jnp.int32), -1)
    for p in range(SHARDS):
        asked[p] = jnp.broadcast_to(wide[p : p + 1], (8, 128))

    greet(
        [(dp, table_peer(k)) for k in range(1, SHARDS)]
        + [(z_peer(k) * NY + y, shard) for k in range(1, nz)]
        + [along_y(k) for k in range(1, NY)]
    )

    started = []

    def start(copy):
        copy.start()
        started.append(copy)
        return copy

    def drain():
        for copy in started:
            copy.wait_send()
        started.clear()

    local[1].wait()
    local[2].wait()
    for k in across_z:
        q = z_peer(k)
        block = wout.at[x, core, :, z, y]
        start(remote(block, block, z_s.at[k], z_r.at[z], (q * NY + y, shard)))

    for k in across_table:
        p = table_peer(k)
        start(remote(asked.at[p], held.at[shard], req_s.at[k], req_r.at[shard], (dp, p)))
    held[shard] = asked[shard]

    local[3].wait()
    for k in reversed(across_table):
        p = table_peer(k)
        remote(asked.at[p], held.at[p], req_s.at[k], req_r.at[p], (dp, p)).wait_recv()
    for group in range(2):
        rows = dot(slot_rows(held, group), table_ref[...], ((0,), (0,)))
        found[4 * group : 4 * group + 4] = rows.astype(bf16).reshape(4, MICRO, CAP, columns)
    for k in across_table:
        p = table_peer(k)
        start(remote(found.at[p], fetched.at[shard], fnd_s.at[k], fnd_r.at[shard], (dp, p)))
    fetched[shard] = found[shard]

    for k in reversed(across_z):
        q = z_peer(k)
        block = wout.at[x, core, :, q, y]
        remote(block, block, z_s.at[k], z_r.at[q], (q * NY + y, shard)).wait_recv()

    whole, low, high = pl.ds(0, nz), pl.ds(0, half), pl.ds(half, half)
    views = (
        lambda i, zs: wout.at[x, core, 0, zs, i],
        lambda i, zs: wout.at[i, core, 1, zs, y],
        lambda i, zs: wout.at[i, core, 0, zs],
        lambda i, zs: wout.at[:, core, 1, zs, i],
    )
    spots = (y, x, x, y)
    steps = (along_y, along_x, along_x, along_y)

    def link(ring, which, offset, zs, to):
        block = views[ring](lax.rem(spots[ring] + offset, 4), zs)
        return remote(
            block, block, ring_s.at[ring, which], ring_r.at[ring, which], steps[ring](to)
        )

    def ring_first(ring):
        start(link(ring, 0, 0, whole, 1))
        start(link(ring, 1, 0, whole, 3))

    def ring_second(ring):
        link(ring, 0, 3, whole, 1).wait_recv()
        start(link(ring, 2, 3, low, 1))
        link(ring, 1, 1, whole, 3).wait_recv()
        start(link(ring, 3, 1, high, 3))

    def ring_third(ring):
        link(ring, 2, 2, low, 1).wait_recv()
        link(ring, 3, 2, high, 3).wait_recv()

    def across(ring, offset, mine=True):
        i = lax.rem(spots[ring] + offset, 4)
        c = core if mine else other
        block = wout.at[i, c, 0] if ring == 2 else wout.at[:, c, 1, :, i]
        s = (ring - 2) * 4 + offset
        return remote(block, block, core_s.at[s], core_r.at[s], (dp, x * 2 + other))

    for ring in (0, 1):
        ring_first(ring)
    for ring in (0, 1):
        ring_second(ring)
    for ring in (0, 1):
        ring_third(ring)
    for ring in (2, 3):
        ring_first(ring)
        start(across(ring, 0))

    for k in reversed(across_table):
        p = table_peer(k)
        remote(found.at[p], fetched.at[p], fnd_s.at[k], fnd_r.at[p], (dp, p)).wait_recv()
    for copy in local[7:]:
        copy.wait()
    count = seg_ref.shape[2]
    slots = SHARDS * CAP
    collect, expand, share = [], [], []
    number = lax.broadcasted_iota(jnp.int32, (slots, count), 0)
    user = lax.broadcasted_iota(jnp.int32, (8, count), 0)
    causal = lax.broadcasted_iota(jnp.int32, (count, count), 0) >= lax.broadcasted_iota(
        jnp.int32, (count, count), 1
    )
    for m in range(MICRO):
        hot = jnp.where(number == slot_ref[m], 1.0, 0.0)
        collect.append(hot.astype(bf16))
        expand.append(jnp.transpose(hot).astype(bf16))
        belongs = jnp.where(user == seg_ref[m], 1.0, 0.0).astype(bf16)
        same = dot(belongs, belongs, ((0,), (0,)))
        history = jnp.sum(same, axis=1, keepdims=True)
        share.append(jnp.where(causal, same, 0.0) / history)
    rows = jnp.concatenate(
        [fetched[:, m].reshape(slots, columns) for m in range(MICRO)], axis=0
    ).astype(f32)
    normed, factor = normalise(rows)
    given = normed.astype(bf16)
    lane = lax.broadcasted_iota(jnp.int32, (1, columns), 1)
    deep = lax.broadcasted_iota(jnp.int32, (columns, 256), 0)
    for i in range(NY):
        j = lane[:, 256 * i : 256 * i + 256]
        origin = ((j // 16) % nz) * (NY * 16) + (j // (16 * nz)) * 16 + j % 16
        order = jnp.where(deep == origin, 1.0, 0.0).astype(bf16)
        given_y[:, 256 * i : 256 * i + 256] = dot(given, order).astype(bf16)

    def finish(flat, at):
        at = pl.ds(pl.multiple_of(at, 128), 128)
        sig = sigmoid(flat)
        slope[:, at] = sig * (1.0 + flat * (1.0 - sig))
        top = (flat * sig).astype(bf16)
        for m in range(MICRO):
            tokens_of = dot(expand[m], top[m * slots : (m + 1) * slots])
            flow[m * count : (m + 1) * count, at] = tokens_of.astype(bf16)

    def project_x(offset, c):
        i = lax.rem(x + offset, NX)
        finish(dot(given, wout[i, c, 0].reshape(columns, 128)), i * 512 + c * 256)

    def project_y(offset, which):
        i, c = y_peer(offset), (core, other)[which]
        block = jnp.concatenate([wout[n, c, 1, :, i].reshape(16 * nz, 128) for n in range(NX)], axis=1)
        mine = given_y[:, pl.ds(pl.multiple_of(i * 256, 256), 256)]
        if offset == 0:
            sums[which] = dot(mine, block)
        else:
            sums[which] += dot(mine, block)

    def project_rest(which):
        c = (core, other)[which]
        for n in range(NX):
            finish(sums[which, :, 128 * n : 128 * n + 128], n * 512 + c * 256 + 128)

    def project(offsets):
        for offset in offsets:
            project_x(offset, core)
            project_y(offset, 0)
        if offsets[-1] == 2:
            project_rest(0)
        for offset in offsets:
            for ring in (2, 3):
                across(ring, offset, mine=False).wait_recv()
            project_x(offset, other)
            project_y(offset, 1)
        if offsets[-1] == 2:
            project_rest(1)

    project((0,))
    for ring in (2, 3):
        ring_second(ring)
        start(across(ring, 3))
        start(across(ring, 1))
    project((3, 1))

    i32 = jnp.int32
    live = lax.broadcasted_iota(i32, (DCAP, 64), 0) < tally_ref[...]
    aims = jnp.where(live, target_ref[...] + 1, 0).astype(f32).astype(bf16)
    lane = lax.broadcasted_iota(i32, (64, 64), 1)
    deep = lax.broadcasted_iota(i32, (64, 64), 0)
    here = jnp.where(deep == (lane // DCAP) * SHARDS + shard, 1.0, 0.0).astype(bf16)
    aims = dot(aims, here)
    lane = lax.broadcasted_iota(i32, (DCAP, 64), 1) % DCAP
    deep = lax.broadcasted_iota(i32, (DCAP, 64), 0)
    aims = jnp.sum(jnp.where(lane == deep, aims, 0.0), axis=0, keepdims=True).astype(i32) - 1
    number = lax.broadcasted_iota(i32, (128, 64), 0)
    pick = jnp.where(number == aims, 1.0, 0.0)
    tally = jnp.sum(pick, axis=1, keepdims=True)
    pick = pick.astype(bf16)
    lane = lax.broadcasted_iota(i32, (64, 64), 1)
    deep = lax.broadcasted_iota(i32, (64, 64), 0)
    limit = jnp.where(lane == shard * SHARDS + deep // DCAP, tally_ref[...].astype(f32), 0.0)
    limit = jnp.sum(limit, axis=1, keepdims=True)
    row = (lax.broadcasted_iota(i32, (64, 1), 0) % DCAP).astype(f32)
    scale = 1.0 / (1.0 + tally)
    scale = jnp.concatenate([scale[:64], jnp.where(row < limit, 0.0, scale[64:])], axis=0)

    for ring in (2, 3):
        ring_third(ring)
        start(across(ring, 2))

    for copy in local[4:7]:
        copy.wait()
    for p in range(SHARDS):
        line = slice(64 + DCAP * p, 64 + DCAP * p + DCAP)
        mom_send[p] = jnp.concatenate([first_ref[line], second_ref[line]], axis=0).astype(bf16)
    project((2,))
    for k in across_table:
        p = table_peer(k)
        start(remote(mom_send.at[p], mom_got.at[shard], m_s.at[k], m_r.at[shard], (dp, p)))
    mom_got[shard] = mom_send[shard]

    width = 512
    head = width // HEADS

    def weight(i):
        sides = [wout[i // 2, i % 2, g].reshape(columns, 128) for g in range(2)]
        return jnp.concatenate(sides, axis=1)

    def slot_send(piece, src, to, k, p):
        m = min(piece, 1)
        over = slice(None) if piece == 0 else pl.ds((piece - 1) * columns // 2, columns // 2)
        return remote(
            grads.at[src, m, :, over],
            arrived.at[to, m, :, over],
            a_s.at[piece, k],
            a_r.at[piece, to],
            (dp, p),
        )

    factor_scale = head ** (-0.5)
    for m in range(MICRO):
        span = slice(m * count, (m + 1) * count)
        part = slice(m * slots, (m + 1) * slots)
        for h in range(HEADS):
            values = flow[span, width + h * head : width + (h + 1) * head]
            queries = flow[span, 2 * width + h * head : 2 * width + (h + 1) * head]
            keys = flow[span, 3 * width + h * head : 3 * width + (h + 1) * head]
            scores = dot(queries, keys, ((1,), (1,))) * factor_scale
            sig = sigmoid(scores)
            shared = share[m] * sig
            weights = (scores * shared).astype(bf16)
            attn[h] = weights
            attn_slope[h] = shared * (1.0 + scores * (1.0 - sig)) * factor_scale
            mixed[:, h * head : (h + 1) * head] = dot(weights, values)
        level, spread = normalise(mixed[...])
        upstream = cot_ref[m].astype(f32)
        back[:, :width] = (upstream * level).astype(bf16)
        grad_mixed = normalise_back(
            upstream * flow[span, :width].astype(f32), level, spread
        ).astype(bf16)
        for h in range(HEADS):
            values = flow[span, width + h * head : width + (h + 1) * head]
            queries = flow[span, 2 * width + h * head : 2 * width + (h + 1) * head]
            keys = flow[span, 3 * width + h * head : 3 * width + (h + 1) * head]
            grad_out = grad_mixed[:, h * head : (h + 1) * head]
            grad_attn = dot(grad_out, values, ((1,), (1,))).astype(bf16)
            grad_scores = (grad_attn.astype(f32) * attn_slope[h]).astype(bf16)
            at = width + h * head
            back[:, at : at + head] = dot(attn[h], grad_out, ((0,), (0,))).astype(bf16)
            at = 2 * width + h * head
            back[:, at : at + head] = dot(grad_scores, keys).astype(bf16)
            at = 3 * width + h * head
            back[:, at : at + head] = dot(grad_scores, queries, ((0,), (0,))).astype(bf16)
        grad_normed = jnp.zeros((slots, columns), f32)
        for i in range(8):
            side = slice(256 * i, 256 * i + 256)
            grad_flat = (dot(collect[m], back[:, side]) * slope[part, side]).astype(bf16)
            grad_normed = grad_normed + dot(grad_flat, weight(i), ((1,), (1,)))
        grad_normed = grad_normed.astype(bf16).astype(f32)
        slot_grad = normalise_back(grad_normed, normed[part], factor[part]).astype(bf16)
        grads[:, m] = slot_grad.reshape(SHARDS, CAP, columns)
        for piece in ((0,), (1, 2))[m]:
            for k in across_table:
                start(slot_send(piece, table_peer(k), shard, k, table_peer(k)))
    arrived[shard] = grads[shard]

    asks = [slot_rows(held, group) for group in range(2)]
    side = columns // 2
    tiles = nz // 2
    lines = blocks // 2

    def half_sums(h):
        for piece in ((0, 1), (2,))[h]:
            for k in reversed(across_table):
                p = table_peer(k)
                slot_send(piece, p, p, k, p).wait_recv()
        dense = jnp.zeros((128, side), f32)
        for group in range(2):
            came = arrived[4 * group : 4 * group + 4, :, :, h * side : (h + 1) * side]
            dense = dense + dot(asks[group], came.reshape(128, side))
        dense = dense.astype(bf16)
        for part in range(NY):
            for r in range(2):
                for b in range(lines):
                    at = part * 32 + r * 16
                    y_send[part, h * tiles + r * lines + b] = dense[
                        at : at + 16, b * 128 : b * 128 + 128
                    ]

    def half_y(h, q, to, k):
        part = pl.ds(h * tiles, tiles)
        return remote(
            y_send.at[q, part], y_got.at[to, part], ry_s.at[h, k], ry_r.at[h, to], along_y(k)
        )

    def half_z(h, j):
        q = lax.rem(z + j, tiles) + h * tiles
        return remote(z_send.at[q], z_got.at[z], rz_s.at[h, j], rz_r.at[z], (q * NY + y, shard))

    around = [tiles // 2]
    for j in range(tiles // 2 - 1, 0, -1):
        around += [j, tiles - j]

    for h in range(2):
        half_sums(h)
        for k in across_y:
            start(half_y(h, y_peer(k), y, k))
    drain()
    for h in range(2):
        part = slice(h * tiles, (h + 1) * tiles)
        y_sum = y_send[y, part].astype(f32)
        for k in reversed(across_y):
            q = y_peer(k)
            half_y(h, q, q, k).wait_recv()
            y_sum = y_sum + y_got[q, part].astype(f32)
        z_send[part] = y_sum.astype(bf16)
        for j in around:
            start(half_z(h, j))

        @pl.when(z // tiles != h)
        def _():
            half_z(h, 0).start()

    z_sum = z_send[z].astype(f32)
    for k in reversed(across_z):
        q = z_peer(k)
        remote(z_send.at[q], z_got.at[q], rz_s.at[0, 0], rz_r.at[q], (q * NY + y, shard)).wait_recv()
        z_sum = z_sum + z_got[q].astype(f32)
    total[y, z] = z_sum.astype(bf16)

    for k in across_z:
        q = z_peer(k)
        block = total.at[y, z]
        start(remote(block, block, gz_s.at[k], gz_r.at[z], (q * NY + y, shard)))
    def tile_of(q):
        block = total.at[y, q]
        return remote(block, block, gz_s.at[1], gz_r.at[q], (q * NY + y, shard))

    def out_y(h, q, k):
        block = total.at[q, pl.ds(h * tiles, tiles)]
        return remote(block, block, gy_s.at[h, k], gy_r.at[h, q], along_y(k))

    for h in range(2):
        for j in reversed(around):
            tile_of(lax.rem(z + j, tiles) + h * tiles).wait_recv()

        @pl.when(z // tiles != h)
        def _():
            tile_of(lax.rem(z, tiles) + h * tiles).wait_recv()

        for k in across_y:
            start(out_y(h, y, k))

    for k in reversed(across_table):
        p = table_peer(k)
        remote(mom_send.at[p], mom_got.at[p], m_s.at[k], m_r.at[p], (dp, p)).wait_recv()
    def rep_out(h, src, to, k, p):
        return remote(
            rep_send.at[h, src], rep_got.at[h, to], r_s.at[h, k], r_r.at[h, to], (dp, p)
        )

    for h in range(2):
        for k in reversed(across_y):
            out_y(h, y_peer(k), k).wait_recv()
        grad = [
            jnp.concatenate(
                [total[n // 2, h * tiles + (n % 2) * lines + b] for b in range(lines)], axis=1
            ).astype(f32)
            for n in range(8)
        ]
        for p in range(SHARDS):
            own = grad[4 + p // 2][(p % 2) * 8 : (p % 2) * 8 + 8]
            rep_send[h, p] = jnp.concatenate(
                [own[:, : side // 2], own[:, side // 2 :]], axis=0
            ).astype(bf16)
        for k in across_table:
            p = table_peer(k)
            start(rep_out(h, p, shard, k, p))
        rep_got[h, shard] = rep_send[h, shard]
        over = slice(h * side, (h + 1) * side)
        for n in range(8):
            span = slice(16 * n, 16 * n + 16)
            first_out[span, over] = beta_one * first_ref[span, over] + (1.0 - beta_one) * grad[n]
            second_out[span, over] = beta_two * second_ref[span, over] + (1.0 - beta_two) * (
                grad[n] * grad[n]
            )
    drain()
    for h in range(2):
        over = slice(h * side, (h + 1) * side)
        for k in reversed(across_table):
            p = table_peer(k)
            rep_out(h, p, p, k, p).wait_recv()
        rep_first, rep_second = [], []
        for p in range(SHARDS):
            halves = rep_got[h, p].astype(f32)
            grad = jnp.concatenate([halves[:8], halves[8:]], axis=1)
            moments = mom_got[p, :, over].astype(f32)
            rep_first.append(beta_one * moments[:8] + (1.0 - beta_one) * grad)
            rep_second.append(beta_two * moments[8:] + (1.0 - beta_two) * (grad * grad))
        rep_first = dot(pick, jnp.concatenate(rep_first, axis=0).astype(bf16))
        rep_second = dot(pick, jnp.concatenate(rep_second, axis=0).astype(bf16))
        first_out[:, over] = (first_out[:, over] + rep_first) * scale
        second_out[:, over] = (second_out[:, over] + rep_second) * scale
    for h in range(2):

        @pl.when(z // tiles != h)
        def _():
            half_z(h, 0).wait_send()

    for copy in started:
        copy.wait_send()


def body(
    nz,
    token_slot,
    seg_ids,
    req_rows,
    cotangent,
    uvqk_weight,
    table,
    first_moment,
    second_moment,
    dup_count,
    dup_target,
):
    columns = table.shape[1]
    count = token_slot.shape[2]
    tokens = MICRO * count
    slots = SHARDS * CAP
    vmem = pl.BlockSpec(memory_space=pltpu.VMEM)
    hbm = pl.BlockSpec(memory_space=pl.ANY)
    dma = pltpu.SemaphoreType.DMA
    bf16, f32, i32 = jnp.bfloat16, jnp.float32, jnp.int32

    tiles = 2 * columns // 128
    first, second = pl.pallas_call(
        functools.partial(whole_kernel, nz),
        out_shape=(
            jax.ShapeDtypeStruct(table.shape, f32),
            jax.ShapeDtypeStruct(table.shape, f32),
        ),
        in_specs=[hbm] * 10,
        out_specs=(vmem,) * 2,
        scratch_shapes=[
            pltpu.VMEM(req_rows.shape, i32),
            pltpu.VMEM(token_slot.shape, i32),
            pltpu.VMEM(seg_ids.shape, i32),
            pltpu.VMEM((1, SHARDS * SHARDS), i32),
            pltpu.VMEM((DCAP, SHARDS * SHARDS), i32),
            pltpu.VMEM((SHARDS, 8, 128), i32),
            pltpu.VMEM((SHARDS, 8, 128), i32),
            pltpu.VMEM(table.shape, bf16),
            pltpu.VMEM((NX, 2, 2, nz, NY, 16, 128), bf16),
            pltpu.VMEM((MICRO, count, 512), bf16),
            pltpu.VMEM(table.shape, f32),
            pltpu.VMEM(table.shape, f32),
            pltpu.VMEM((SHARDS, MICRO, CAP, columns), bf16),
            pltpu.VMEM((SHARDS, MICRO, CAP, columns), bf16),
            pltpu.VMEM((MICRO * slots, columns), bf16),
            pltpu.VMEM((2, MICRO * slots, 512), f32),
            pltpu.VMEM((MICRO * slots, 2048), f32),
            pltpu.VMEM((tokens, 2048), bf16),
            pltpu.VMEM((HEADS, count, count), bf16),
            pltpu.VMEM((HEADS, count, count), f32),
            pltpu.VMEM((count, 512), f32),
            pltpu.VMEM((count, 2048), bf16),
            pltpu.VMEM((SHARDS, MICRO, CAP, columns), bf16),
            pltpu.VMEM((SHARDS, MICRO, CAP, columns), bf16),
            pltpu.VMEM((NY, tiles, 16, 128), bf16),
            pltpu.VMEM((NY, tiles, 16, 128), bf16),
            pltpu.VMEM((tiles, 16, 128), bf16),
            pltpu.VMEM((tiles, 16, 128), bf16),
            pltpu.VMEM((NY, tiles, 16, 128), bf16),
            pltpu.VMEM((SHARDS, 16, columns), bf16),
            pltpu.VMEM((SHARDS, 16, columns), bf16),
            pltpu.VMEM((2, SHARDS, 16, columns // 4), bf16),
            pltpu.VMEM((2, SHARDS, 16, columns // 4), bf16),
            dma((11,)),
            dma((SHARDS,)),
            dma((SHARDS,)),
            dma((SHARDS,)),
            dma((SHARDS,)),
            dma((nz,)),
            dma((nz,)),
            dma((4, 4)),
            dma((4, 4)),
            dma((8,)),
            dma((8,)),
            dma((3, SHARDS)),
            dma((3, SHARDS)),
            dma((2, NY)),
            dma((2, NY)),
            dma((2, nz // 2)),
            dma((nz,)),
            dma((nz,)),
            dma((nz,)),
            dma((2, NY)),
            dma((2, NY)),
            dma((SHARDS,)),
            dma((SHARDS,)),
            dma((2, SHARDS)),
            dma((2, SHARDS)),
        ],
        compiler_params=pltpu.CompilerParams(
            collective_id=0, has_side_effects=True, vmem_limit_bytes=63 << 20
        ),
        name="whole",
    )(
        req_rows,
        token_slot,
        seg_ids,
        dup_count[None, :],
        dup_target.T,
        table,
        uvqk_weight,
        cotangent,
        first_moment,
        second_moment,
    )
    keep = second > 0.0
    new_first = jnp.where(keep, first, 0.0)
    new_second = jnp.where(keep, second, 0.0)
    update = table.astype(f32) - learn_rate * new_first / (jnp.sqrt(new_second) + adam_eps)
    return (jnp.where(keep, update, 0.0).astype(bf16), new_first, new_second)


def solution(mesh):
    placed = (
        P(None, ("dp", "table"), None),
        P(None, ("dp", "table"), None),
        P(None, ("dp", "table"), None),
        P(None, ("dp", "table"), None),
        P("dp", None),
        P("table", None),
        P("table", None),
        P("table", None),
        P(),
        P(),
    )
    return jax.shard_map(
        functools.partial(body, mesh.shape["dp"] // NY),
        mesh=mesh,
        in_specs=placed,
        out_specs=(P("table", None), P("table", None), P("table", None)),
        check_vma=False,
    )
```

```python
import functools

import jax
import jax.numpy as jnp
from jax import lax
from jax.experimental import pallas as pl
from jax.experimental.pallas import tpu as pltpu
from jax.sharding import PartitionSpec as P

MESH = pl.DeviceIdType.MESH
HEADS = 4
MICRO = 2
NX = 4
NY = 4
SHARDS = 8
CAP = 16
DCAP = 8

beta_one = 0.9
beta_two = 0.999
learn_rate = 0.1
adam_eps = 1e-08
norm_eps = 1e-05


def dot(a, b, dims=((1,), (0,))):
    return lax.dot_general(a, b, (dims, ((), ())), preferred_element_type=jnp.float32)


def place():
    dp = lax.axis_index("dp")
    shard = lax.axis_index("table")
    return dp // NY, dp % NY, shard // 2, shard % 2, dp, shard


def greet(peers):
    barrier = pltpu.get_barrier_semaphore()
    for peer in peers:
        pl.semaphore_signal(barrier, inc=1, device_id=peer, device_id_type=MESH)
    return barrier, len(peers)


def remote(src, dst, send, recv, peer):
    return pltpu.make_async_remote_copy(
        src_ref=src, dst_ref=dst, send_sem=send, recv_sem=recv, device_id=peer, device_id_type=MESH
    )


def slot_rows(held_ref, group):
    rows = held_ref[4 * group]
    for peer in range(1, 4):
        rows = jnp.maximum(rows, held_ref[4 * group + peer])
    number = lax.broadcasted_iota(jnp.int32, (128, 128), 0)
    return jnp.where(number == rows[0:1], 1.0, 0.0).astype(jnp.bfloat16)


def normalise(values):
    center = jnp.mean(values, axis=-1, keepdims=True)
    shifted = values - center
    spread = jnp.mean(shifted * shifted, axis=-1, keepdims=True)
    factor = lax.rsqrt(spread + norm_eps)
    return shifted * factor, factor


def normalise_back(grad, normed, factor):
    grad_mean = jnp.mean(grad, axis=-1, keepdims=True)
    along = jnp.mean(grad * normed, axis=-1, keepdims=True)
    return factor * (grad - grad_mean - normed * along)


def sigmoid(values):
    return 0.5 * jnp.tanh(0.5 * values) + 0.5


def whole_kernel(
    nz,
    req_hbm,
    slot_hbm,
    seg_hbm,
    tally_hbm,
    target_hbm,
    table_hbm,
    w_hbm,
    cot_hbm,
    first_hbm,
    second_hbm,
    first_out,
    second_out,
    req_ref,
    slot_ref,
    seg_ref,
    tally_ref,
    target_ref,
    asked,
    held,
    table_ref,
    wout,
    cot_ref,
    first_ref,
    second_ref,
    found,
    fetched,
    given_y,
    sums,
    slope,
    flow,
    attn,
    attn_slope,
    mixed,
    back,
    grads,
    arrived,
    y_send,
    y_got,
    z_send,
    z_got,
    total,
    mom_send,
    mom_got,
    rep_send,
    rep_got,
    local_s,
    req_s,
    req_r,
    fnd_s,
    fnd_r,
    z_s,
    z_r,
    ring_s,
    ring_r,
    core_s,
    core_r,
    a_s,
    a_r,
    ry_s,
    ry_r,
    rz_s,
    rz_r,
    gz_s,
    gz_r,
    gy_s,
    gy_r,
    m_s,
    m_r,
    r_s,
    r_r,
):
    z, y, x, core, dp, shard = place()
    other = 1 - core
    half = nz // 2
    columns = table_ref.shape[1]
    blocks = columns // 128
    f32, bf16 = jnp.float32, jnp.bfloat16

    def table_peer(k):
        return lax.rem(shard + k, SHARDS)

    def z_peer(k):
        return lax.rem(z + k, nz)

    def y_peer(k):
        return lax.rem(y + k, NY)

    def along_y(k):
        return (z * NY + y_peer(k), shard)

    def along_x(k):
        return (dp, lax.rem(x + k, NX) * 2 + core)

    across_table = (4, 3, 5, 2, 6, 1, 7)
    across_z = [nz // 2]
    for k in range(nz // 2 - 1, 0, -1):
        across_z += [k, nz - k]
    across_y = (2, 1, 3)

    barrier = greet(
        [(dp, table_peer(k)) for k in range(1, SHARDS)]
        + [(z_peer(k) * NY + y, shard) for k in range(1, nz)]
        + [along_y(k) for k in range(1, NY)]
    )

    local = [(req_hbm, req_ref)]
    for g in range(2):
        part = pl.ds(pl.multiple_of(shard * 256 + g * 128, 128), 128)
        local.append((w_hbm.at[:, part], wout.at[x, core, g, z, y]))
    local += [
        (table_hbm, table_ref),
        (cot_hbm, cot_ref),
        (first_hbm, first_ref),
        (second_hbm, second_ref),
        (slot_hbm, slot_ref),
        (seg_hbm, seg_ref),
        (tally_hbm, tally_ref),
        (target_hbm, target_ref),
    ]
    local = [pltpu.make_async_copy(a, b, local_s.at[i]) for i, (a, b) in enumerate(local)]
    for copy in local:
        copy.start()

    pl.semaphore_wait(*barrier)

    started = []

    def start(copy):
        copy.start()
        started.append(copy)
        return copy

    def drain():
        for copy in started:
            copy.wait_send()
        started.clear()

    local[1].wait()
    local[2].wait()
    for k in across_z:
        q = z_peer(k)
        block = wout.at[x, core, :, z, y]
        start(remote(block, block, z_s.at[k], z_r.at[z], (q * NY + y, shard)))

    local[0].wait()
    lane = lax.broadcasted_iota(jnp.int32, (CAP, 128), 1) % 32
    deep = lax.broadcasted_iota(jnp.int32, (CAP, 128), 0)
    wide = jnp.zeros((SHARDS, 128), f32)
    for m in range(MICRO):
        spot = jnp.where(lane == deep + m * CAP, 1.0, 0.0).astype(bf16)
        wide = wide + dot(req_ref[m].astype(f32).astype(bf16), spot)
    mine = lax.broadcasted_iota(jnp.int32, (SHARDS, 128), 1) // 32 == lax.rem(shard, 4)
    wide = jnp.where(mine, wide.astype(jnp.int32), -1)
    for p in range(SHARDS):
        asked[p] = jnp.broadcast_to(wide[p : p + 1], (8, 128))
    for k in across_table:
        p = table_peer(k)
        start(remote(asked.at[p], held.at[shard], req_s.at[k], req_r.at[shard], (dp, p)))
    held[shard] = asked[shard]

    local[3].wait()
    for k in reversed(across_table):
        p = table_peer(k)
        remote(asked.at[p], held.at[p], req_s.at[k], req_r.at[p], (dp, p)).wait_recv()
    for group in range(2):
        rows = dot(slot_rows(held, group), table_ref[...], ((0,), (0,)))
        found[4 * group : 4 * group + 4] = rows.astype(bf16).reshape(4, MICRO, CAP, columns)
    for k in across_table:
        p = table_peer(k)
        start(remote(found.at[p], fetched.at[shard], fnd_s.at[k], fnd_r.at[shard], (dp, p)))
    fetched[shard] = found[shard]

    for k in reversed(across_z):
        q = z_peer(k)
        block = wout.at[x, core, :, q, y]
        remote(block, block, z_s.at[k], z_r.at[q], (q * NY + y, shard)).wait_recv()

    whole, low, high = pl.ds(0, nz), pl.ds(0, half), pl.ds(half, half)
    views = (
        lambda i, zs: wout.at[x, core, 0, zs, i],
        lambda i, zs: wout.at[i, core, 1, zs, y],
        lambda i, zs: wout.at[i, core, 0, zs],
        lambda i, zs: wout.at[:, core, 1, zs, i],
    )
    spots = (y, x, x, y)
    steps = (along_y, along_x, along_x, along_y)

    def link(ring, which, offset, zs, to):
        block = views[ring](lax.rem(spots[ring] + offset, 4), zs)
        return remote(
            block, block, ring_s.at[ring, which], ring_r.at[ring, which], steps[ring](to)
        )

    def ring_first(ring):
        start(link(ring, 0, 0, whole, 1))
        start(link(ring, 1, 0, whole, 3))

    def ring_second(ring):
        link(ring, 0, 3, whole, 1).wait_recv()
        start(link(ring, 2, 3, low, 1))
        link(ring, 1, 1, whole, 3).wait_recv()
        start(link(ring, 3, 1, high, 3))

    def ring_third(ring):
        link(ring, 2, 2, low, 1).wait_recv()
        link(ring, 3, 2, high, 3).wait_recv()

    def across(ring, offset, mine=True):
        i = lax.rem(spots[ring] + offset, 4)
        c = core if mine else other
        block = wout.at[i, c, 0] if ring == 2 else wout.at[:, c, 1, :, i]
        s = (ring - 2) * 4 + offset
        return remote(block, block, core_s.at[s], core_r.at[s], (dp, x * 2 + other))

    def middle(ring, which, offset):
        block = views[ring](lax.rem(spots[ring] + offset, 4), whole)
        return remote(
            block, block, ring_s.at[ring, which], ring_r.at[ring, which], steps[ring](which)
        )

    for which in (2, 1, 3):
        for ring in (0, 1):
            start(middle(ring, which, 0))
    for which in (1, 3, 2):
        for ring in (0, 1):
            middle(ring, which, 4 - which).wait_recv()
    for ring in (2, 3):
        ring_first(ring)
        start(across(ring, 0))

    for k in reversed(across_table):
        p = table_peer(k)
        remote(found.at[p], fetched.at[p], fnd_s.at[k], fnd_r.at[p], (dp, p)).wait_recv()
    for copy in local[7:]:
        copy.wait()
    count = seg_ref.shape[2]
    slots = SHARDS * CAP
    collect, expand, share = [], [], []
    number = lax.broadcasted_iota(jnp.int32, (slots, count), 0)
    user = lax.broadcasted_iota(jnp.int32, (8, count), 0)
    causal = lax.broadcasted_iota(jnp.int32, (count, count), 0) >= lax.broadcasted_iota(
        jnp.int32, (count, count), 1
    )
    for m in range(MICRO):
        hot = jnp.where(number == slot_ref[m], 1.0, 0.0)
        collect.append(hot.astype(bf16))
        expand.append(jnp.transpose(hot).astype(bf16))
        belongs = jnp.where(user == seg_ref[m], 1.0, 0.0).astype(bf16)
        same = dot(belongs, belongs, ((0,), (0,)))
        history = jnp.sum(same, axis=1, keepdims=True)
        share.append(jnp.where(causal, same, 0.0) / history)
    rows = jnp.concatenate(
        [fetched[:, m].reshape(slots, columns) for m in range(MICRO)], axis=0
    ).astype(f32)
    normed, factor = normalise(rows)
    given = normed.astype(bf16)
    lane = lax.broadcasted_iota(jnp.int32, (1, columns), 1)
    deep = lax.broadcasted_iota(jnp.int32, (columns, 256), 0)
    for i in range(NY):
        j = lane[:, 256 * i : 256 * i + 256]
        origin = ((j // 16) % nz) * (NY * 16) + (j // (16 * nz)) * 16 + j % 16
        order = jnp.where(deep == origin, 1.0, 0.0).astype(bf16)
        given_y[:, 256 * i : 256 * i + 256] = dot(given, order).astype(bf16)

    def finish(flat, at):
        at = pl.ds(pl.multiple_of(at, 128), 128)
        sig = sigmoid(flat)
        slope[:, at] = sig * (1.0 + flat * (1.0 - sig))
        top = (flat * sig).astype(bf16)
        for m in range(MICRO):
            tokens_of = dot(expand[m], top[m * slots : (m + 1) * slots])
            flow[m * count : (m + 1) * count, at] = tokens_of.astype(bf16)

    def project_x(offset, c):
        i = lax.rem(x + offset, NX)
        finish(dot(given, wout[i, c, 0].reshape(columns, 128)), i * 512 + c * 256)

    def project_y(offset, which):
        i, c = y_peer(offset), (core, other)[which]
        block = jnp.concatenate([wout[n, c, 1, :, i].reshape(16 * nz, 128) for n in range(NX)], axis=1)
        mine = given_y[:, pl.ds(pl.multiple_of(i * 256, 256), 256)]
        if offset == 0:
            sums[which] = dot(mine, block)
        else:
            sums[which] += dot(mine, block)

    def project_rest(which):
        c = (core, other)[which]
        for n in range(NX):
            finish(sums[which, :, 128 * n : 128 * n + 128], n * 512 + c * 256 + 128)

    def project(offsets):
        for offset in offsets:
            project_x(offset, core)
            project_y(offset, 0)
        if offsets[-1] == 2:
            project_rest(0)
        for offset in offsets:
            for ring in (2, 3):
                across(ring, offset, mine=False).wait_recv()
            project_x(offset, other)
            project_y(offset, 1)
        if offsets[-1] == 2:
            project_rest(1)

    project((0,))
    for ring in (2, 3):
        ring_second(ring)
        start(across(ring, 3))
        start(across(ring, 1))
    project((3, 1))

    i32 = jnp.int32
    live = lax.broadcasted_iota(i32, (DCAP, 64), 0) < tally_ref[...]
    aims = jnp.where(live, target_ref[...] + 1, 0).astype(f32).astype(bf16)
    lane = lax.broadcasted_iota(i32, (64, 64), 1)
    deep = lax.broadcasted_iota(i32, (64, 64), 0)
    here = jnp.where(deep == (lane // DCAP) * SHARDS + shard, 1.0, 0.0).astype(bf16)
    aims = dot(aims, here)
    lane = lax.broadcasted_iota(i32, (DCAP, 64), 1) % DCAP
    deep = lax.broadcasted_iota(i32, (DCAP, 64), 0)
    aims = jnp.sum(jnp.where(lane == deep, aims, 0.0), axis=0, keepdims=True).astype(i32) - 1
    number = lax.broadcasted_iota(i32, (128, 64), 0)
    pick = jnp.where(number == aims, 1.0, 0.0)
    tally = jnp.sum(pick, axis=1, keepdims=True)
    pick = pick.astype(bf16)
    lane = lax.broadcasted_iota(i32, (64, 64), 1)
    deep = lax.broadcasted_iota(i32, (64, 64), 0)
    limit = jnp.where(lane == shard * SHARDS + deep // DCAP, tally_ref[...].astype(f32), 0.0)
    limit = jnp.sum(limit, axis=1, keepdims=True)
    row = (lax.broadcasted_iota(i32, (64, 1), 0) % DCAP).astype(f32)
    scale = 1.0 / (1.0 + tally)
    scale = jnp.concatenate([scale[:64], jnp.where(row < limit, 0.0, scale[64:])], axis=0)

    for ring in (2, 3):
        ring_third(ring)
        start(across(ring, 2))

    for copy in local[4:7]:
        copy.wait()
    for p in range(SHARDS):
        line = slice(64 + DCAP * p, 64 + DCAP * p + DCAP)
        mom_send[p] = jnp.concatenate([first_ref[line], second_ref[line]], axis=0).astype(bf16)
    project((2,))
    for k in across_table:
        p = table_peer(k)
        start(remote(mom_send.at[p], mom_got.at[shard], m_s.at[k], m_r.at[shard], (dp, p)))
    mom_got[shard] = mom_send[shard]

    width = 512
    head = width // HEADS

    def weight(i):
        sides = [wout[i // 2, i % 2, g].reshape(columns, 128) for g in range(2)]
        return jnp.concatenate(sides, axis=1)

    def slot_send(piece, src, to, k, p):
        m = min(piece, 1)
        over = slice(None) if piece == 0 else pl.ds((piece - 1) * columns // 2, columns // 2)
        return remote(
            grads.at[src, m, :, over],
            arrived.at[to, m, :, over],
            a_s.at[piece, k],
            a_r.at[piece, to],
            (dp, p),
        )

    factor_scale = head ** (-0.5)
    for m in range(MICRO):
        span = slice(m * count, (m + 1) * count)
        part = slice(m * slots, (m + 1) * slots)
        for h in range(HEADS):
            values = flow[span, width + h * head : width + (h + 1) * head]
            queries = flow[span, 2 * width + h * head : 2 * width + (h + 1) * head]
            keys = flow[span, 3 * width + h * head : 3 * width + (h + 1) * head]
            scores = dot(queries, keys, ((1,), (1,))) * factor_scale
            sig = sigmoid(scores)
            shared = share[m] * sig
            weights = (scores * shared).astype(bf16)
            attn[h] = weights
            attn_slope[h] = shared * (1.0 + scores * (1.0 - sig)) * factor_scale
            mixed[:, h * head : (h + 1) * head] = dot(weights, values)
        level, spread = normalise(mixed[...])
        upstream = cot_ref[m].astype(f32)
        back[:, :width] = (upstream * level).astype(bf16)
        grad_mixed = normalise_back(
            upstream * flow[span, :width].astype(f32), level, spread
        ).astype(bf16)
        for h in range(HEADS):
            values = flow[span, width + h * head : width + (h + 1) * head]
            queries = flow[span, 2 * width + h * head : 2 * width + (h + 1) * head]
            keys = flow[span, 3 * width + h * head : 3 * width + (h + 1) * head]
            grad_out = grad_mixed[:, h * head : (h + 1) * head]
            grad_attn = dot(grad_out, values, ((1,), (1,))).astype(bf16)
            grad_scores = (grad_attn.astype(f32) * attn_slope[h]).astype(bf16)
            at = width + h * head
            back[:, at : at + head] = dot(attn[h], grad_out, ((0,), (0,))).astype(bf16)
            at = 2 * width + h * head
            back[:, at : at + head] = dot(grad_scores, keys).astype(bf16)
            at = 3 * width + h * head
            back[:, at : at + head] = dot(grad_scores, queries, ((0,), (0,))).astype(bf16)
        grad_normed = jnp.zeros((slots, columns), f32)
        for i in range(8):
            side = slice(256 * i, 256 * i + 256)
            grad_flat = (dot(collect[m], back[:, side]) * slope[part, side]).astype(bf16)
            grad_normed = grad_normed + dot(grad_flat, weight(i), ((1,), (1,)))
        grad_normed = grad_normed.astype(bf16).astype(f32)
        slot_grad = normalise_back(grad_normed, normed[part], factor[part]).astype(bf16)
        grads[:, m] = slot_grad.reshape(SHARDS, CAP, columns)
        for piece in ((0,), (1, 2))[m]:
            for k in across_table:
                start(slot_send(piece, table_peer(k), shard, k, table_peer(k)))
    arrived[shard] = grads[shard]

    asks = [slot_rows(held, group) for group in range(2)]
    side = columns // 2
    tiles = nz // 2
    lines = blocks // 2

    def half_sums(h):
        for piece in ((0, 1), (2,))[h]:
            for k in reversed(across_table):
                p = table_peer(k)
                slot_send(piece, p, p, k, p).wait_recv()
        dense = jnp.zeros((128, side), f32)
        for group in range(2):
            came = arrived[4 * group : 4 * group + 4, :, :, h * side : (h + 1) * side]
            dense = dense + dot(asks[group], came.reshape(128, side))
        dense = dense.astype(bf16)
        for part in range(NY):
            for r in range(2):
                for b in range(lines):
                    at = part * 32 + r * 16
                    y_send[part, h * tiles + r * lines + b] = dense[
                        at : at + 16, b * 128 : b * 128 + 128
                    ]

    def half_y(h, q, to, k):
        part = pl.ds(h * tiles, tiles)
        return remote(
            y_send.at[q, part], y_got.at[to, part], ry_s.at[h, k], ry_r.at[h, to], along_y(k)
        )

    def half_z(h, j):
        q = lax.rem(z + j, tiles) + h * tiles
        return remote(z_send.at[q], z_got.at[z], rz_s.at[h, j], rz_r.at[z], (q * NY + y, shard))

    around = [tiles // 2]
    for j in range(tiles // 2 - 1, 0, -1):
        around += [j, tiles - j]

    for h in range(2):
        half_sums(h)
        for k in across_y:
            start(half_y(h, y_peer(k), y, k))
    drain()
    for h in range(2):
        part = slice(h * tiles, (h + 1) * tiles)
        y_sum = y_send[y, part].astype(f32)
        for k in reversed(across_y):
            q = y_peer(k)
            half_y(h, q, q, k).wait_recv()
            y_sum = y_sum + y_got[q, part].astype(f32)
        z_send[part] = y_sum.astype(bf16)
        for j in around:
            start(half_z(h, j))

        @pl.when(z // tiles != h)
        def _():
            half_z(h, 0).start()

    z_sum = z_send[z].astype(f32)
    for k in reversed(across_z):
        q = z_peer(k)
        remote(z_send.at[q], z_got.at[q], rz_s.at[0, 0], rz_r.at[q], (q * NY + y, shard)).wait_recv()
        z_sum = z_sum + z_got[q].astype(f32)
    total[y, z] = z_sum.astype(bf16)

    for k in across_z:
        q = z_peer(k)
        block = total.at[y, z]
        start(remote(block, block, gz_s.at[k], gz_r.at[z], (q * NY + y, shard)))
    def tile_of(q):
        block = total.at[y, q]
        return remote(block, block, gz_s.at[1], gz_r.at[q], (q * NY + y, shard))

    def out_y(h, q, k):
        block = total.at[q, pl.ds(h * tiles, tiles)]
        return remote(block, block, gy_s.at[h, k], gy_r.at[h, q], along_y(k))

    for h in range(2):
        for j in reversed(around):
            tile_of(lax.rem(z + j, tiles) + h * tiles).wait_recv()

        @pl.when(z // tiles != h)
        def _():
            tile_of(lax.rem(z, tiles) + h * tiles).wait_recv()

        for k in across_y:
            start(out_y(h, y, k))

    for k in reversed(across_table):
        p = table_peer(k)
        remote(mom_send.at[p], mom_got.at[p], m_s.at[k], m_r.at[p], (dp, p)).wait_recv()
    def rep_out(h, src, to, k, p):
        return remote(
            rep_send.at[h, src], rep_got.at[h, to], r_s.at[h, k], r_r.at[h, to], (dp, p)
        )

    for h in range(2):
        for k in reversed(across_y):
            out_y(h, y_peer(k), k).wait_recv()
        grad = [
            jnp.concatenate(
                [total[n // 2, h * tiles + (n % 2) * lines + b] for b in range(lines)], axis=1
            ).astype(f32)
            for n in range(8)
        ]
        for p in range(SHARDS):
            own = grad[4 + p // 2][(p % 2) * 8 : (p % 2) * 8 + 8]
            rep_send[h, p] = jnp.concatenate(
                [own[:, : side // 2], own[:, side // 2 :]], axis=0
            ).astype(bf16)
        for k in across_table:
            p = table_peer(k)
            start(rep_out(h, p, shard, k, p))
        rep_got[h, shard] = rep_send[h, shard]
        over = slice(h * side, (h + 1) * side)
        for n in range(8):
            span = slice(16 * n, 16 * n + 16)
            first_out[span, over] = beta_one * first_ref[span, over] + (1.0 - beta_one) * grad[n]
            second_out[span, over] = beta_two * second_ref[span, over] + (1.0 - beta_two) * (
                grad[n] * grad[n]
            )
    drain()
    for h in range(2):
        over = slice(h * side, (h + 1) * side)
        for k in reversed(across_table):
            p = table_peer(k)
            rep_out(h, p, p, k, p).wait_recv()
        rep_first, rep_second = [], []
        for p in range(SHARDS):
            halves = rep_got[h, p].astype(f32)
            grad = jnp.concatenate([halves[:8], halves[8:]], axis=1)
            moments = mom_got[p, :, over].astype(f32)
            rep_first.append(beta_one * moments[:8] + (1.0 - beta_one) * grad)
            rep_second.append(beta_two * moments[8:] + (1.0 - beta_two) * (grad * grad))
        rep_first = dot(pick, jnp.concatenate(rep_first, axis=0).astype(bf16))
        rep_second = dot(pick, jnp.concatenate(rep_second, axis=0).astype(bf16))
        first_out[:, over] = (first_out[:, over] + rep_first) * scale
        second_out[:, over] = (second_out[:, over] + rep_second) * scale
    for h in range(2):

        @pl.when(z // tiles != h)
        def _():
            half_z(h, 0).wait_send()

    for copy in started:
        copy.wait_send()


def body(
    nz,
    token_slot,
    seg_ids,
    req_rows,
    cotangent,
    uvqk_weight,
    table,
    first_moment,
    second_moment,
    dup_count,
    dup_target,
):
    columns = table.shape[1]
    count = token_slot.shape[2]
    tokens = MICRO * count
    slots = SHARDS * CAP
    vmem = pl.BlockSpec(memory_space=pltpu.VMEM)
    hbm = pl.BlockSpec(memory_space=pl.ANY)
    dma = pltpu.SemaphoreType.DMA
    bf16, f32, i32 = jnp.bfloat16, jnp.float32, jnp.int32

    tiles = 2 * columns // 128
    first, second = pl.pallas_call(
        functools.partial(whole_kernel, nz),
        out_shape=(
            jax.ShapeDtypeStruct(table.shape, f32),
            jax.ShapeDtypeStruct(table.shape, f32),
        ),
        in_specs=[hbm] * 10,
        out_specs=(vmem,) * 2,
        scratch_shapes=[
            pltpu.VMEM(req_rows.shape, i32),
            pltpu.VMEM(token_slot.shape, i32),
            pltpu.VMEM(seg_ids.shape, i32),
            pltpu.VMEM((1, SHARDS * SHARDS), i32),
            pltpu.VMEM((DCAP, SHARDS * SHARDS), i32),
            pltpu.VMEM((SHARDS, 8, 128), i32),
            pltpu.VMEM((SHARDS, 8, 128), i32),
            pltpu.VMEM(table.shape, bf16),
            pltpu.VMEM((NX, 2, 2, nz, NY, 16, 128), bf16),
            pltpu.VMEM((MICRO, count, 512), bf16),
            pltpu.VMEM(table.shape, f32),
            pltpu.VMEM(table.shape, f32),
            pltpu.VMEM((SHARDS, MICRO, CAP, columns), bf16),
            pltpu.VMEM((SHARDS, MICRO, CAP, columns), bf16),
            pltpu.VMEM((MICRO * slots, columns), bf16),
            pltpu.VMEM((2, MICRO * slots, 512), f32),
            pltpu.VMEM((MICRO * slots, 2048), f32),
            pltpu.VMEM((tokens, 2048), bf16),
            pltpu.VMEM((HEADS, count, count), bf16),
            pltpu.VMEM((HEADS, count, count), f32),
            pltpu.VMEM((count, 512), f32),
            pltpu.VMEM((count, 2048), bf16),
            pltpu.VMEM((SHARDS, MICRO, CAP, columns), bf16),
            pltpu.VMEM((SHARDS, MICRO, CAP, columns), bf16),
            pltpu.VMEM((NY, tiles, 16, 128), bf16),
            pltpu.VMEM((NY, tiles, 16, 128), bf16),
            pltpu.VMEM((tiles, 16, 128), bf16),
            pltpu.VMEM((tiles, 16, 128), bf16),
            pltpu.VMEM((NY, tiles, 16, 128), bf16),
            pltpu.VMEM((SHARDS, 16, columns), bf16),
            pltpu.VMEM((SHARDS, 16, columns), bf16),
            pltpu.VMEM((2, SHARDS, 16, columns // 4), bf16),
            pltpu.VMEM((2, SHARDS, 16, columns // 4), bf16),
            dma((11,)),
            dma((SHARDS,)),
            dma((SHARDS,)),
            dma((SHARDS,)),
            dma((SHARDS,)),
            dma((nz,)),
            dma((nz,)),
            dma((4, 4)),
            dma((4, 4)),
            dma((8,)),
            dma((8,)),
            dma((3, SHARDS)),
            dma((3, SHARDS)),
            dma((2, NY)),
            dma((2, NY)),
            dma((2, nz // 2)),
            dma((nz,)),
            dma((nz,)),
            dma((nz,)),
            dma((2, NY)),
            dma((2, NY)),
            dma((SHARDS,)),
            dma((SHARDS,)),
            dma((2, SHARDS)),
            dma((2, SHARDS)),
        ],
        compiler_params=pltpu.CompilerParams(
            collective_id=0, has_side_effects=True, vmem_limit_bytes=63 << 20
        ),
        name="whole",
    )(
        req_rows,
        token_slot,
        seg_ids,
        dup_count[None, :],
        dup_target.T,
        table,
        uvqk_weight,
        cotangent,
        first_moment,
        second_moment,
    )
    keep = second > 0.0
    new_first = jnp.where(keep, first, 0.0)
    new_second = jnp.where(keep, second, 0.0)
    update = table.astype(f32) - learn_rate * new_first / (jnp.sqrt(new_second) + adam_eps)
    return (jnp.where(keep, update, 0.0).astype(bf16), new_first, new_second)


def solution(mesh):
    placed = (
        P(None, ("dp", "table"), None),
        P(None, ("dp", "table"), None),
        P(None, ("dp", "table"), None),
        P(None, ("dp", "table"), None),
        P("dp", None),
        P("table", None),
        P("table", None),
        P("table", None),
        P(),
        P(),
    )
    return jax.shard_map(
        functools.partial(body, mesh.shape["dp"] // NY),
        mesh=mesh,
        in_specs=placed,
        out_specs=(P("table", None), P("table", None), P("table", None)),
        check_vma=False,
    )
```

```python
import functools

import jax
import jax.numpy as jnp
from jax import lax
from jax.experimental import pallas as pl
from jax.experimental.pallas import tpu as pltpu
from jax.sharding import PartitionSpec as P

MESH = pl.DeviceIdType.MESH
HEADS = 4
MICRO = 2
NX = 4
NY = 4
SHARDS = 8
CAP = 16
DCAP = 8

beta_one = 0.9
beta_two = 0.999
learn_rate = 0.1
adam_eps = 1e-08
norm_eps = 1e-05


def dot(a, b, dims=((1,), (0,))):
    return lax.dot_general(a, b, (dims, ((), ())), preferred_element_type=jnp.float32)


def place():
    dp = lax.axis_index("dp")
    shard = lax.axis_index("table")
    return dp // NY, dp % NY, shard // 2, shard % 2, dp, shard


def greet(peers):
    barrier = pltpu.get_barrier_semaphore()
    for peer in peers:
        pl.semaphore_signal(barrier, inc=1, device_id=peer, device_id_type=MESH)
    return barrier, len(peers)


def remote(src, dst, send, recv, peer):
    return pltpu.make_async_remote_copy(
        src_ref=src, dst_ref=dst, send_sem=send, recv_sem=recv, device_id=peer, device_id_type=MESH
    )


def slot_rows(held_ref, group):
    rows = held_ref[4 * group]
    for peer in range(1, 4):
        rows = jnp.maximum(rows, held_ref[4 * group + peer])
    number = lax.broadcasted_iota(jnp.int32, (128, 128), 0)
    return jnp.where(number == rows[0:1], 1.0, 0.0).astype(jnp.bfloat16)


def normalise(values):
    center = jnp.mean(values, axis=-1, keepdims=True)
    shifted = values - center
    spread = jnp.mean(shifted * shifted, axis=-1, keepdims=True)
    factor = lax.rsqrt(spread + norm_eps)
    return shifted * factor, factor


def normalise_back(grad, normed, factor):
    grad_mean = jnp.mean(grad, axis=-1, keepdims=True)
    along = jnp.mean(grad * normed, axis=-1, keepdims=True)
    return factor * (grad - grad_mean - normed * along)


def sigmoid(values):
    return 0.5 * jnp.tanh(0.5 * values) + 0.5


def whole_kernel(
    nz,
    req_hbm,
    slot_hbm,
    seg_hbm,
    tally_hbm,
    target_hbm,
    table_hbm,
    w_hbm,
    cot_hbm,
    first_hbm,
    second_hbm,
    first_out,
    second_out,
    req_ref,
    slot_ref,
    seg_ref,
    tally_ref,
    target_ref,
    asked,
    held,
    table_ref,
    wout,
    cot_ref,
    first_ref,
    second_ref,
    found,
    fetched,
    given_y,
    sums,
    slope,
    flow,
    attn,
    attn_slope,
    mixed,
    back,
    grads,
    arrived,
    y_send,
    y_got,
    z_send,
    z_got,
    total,
    mom_send,
    mom_got,
    rep_send,
    rep_got,
    local_s,
    req_s,
    req_r,
    fnd_s,
    fnd_r,
    z_s,
    z_r,
    ring_s,
    ring_r,
    core_s,
    core_r,
    a_s,
    a_r,
    ry_s,
    ry_r,
    rz_s,
    rz_r,
    gz_s,
    gz_r,
    gy_s,
    gy_r,
    m_s,
    m_r,
    r_s,
    r_r,
):
    z, y, x, core, dp, shard = place()
    other = 1 - core
    half = nz // 2
    columns = table_ref.shape[1]
    blocks = columns // 128
    f32, bf16 = jnp.float32, jnp.bfloat16

    def table_peer(k):
        return lax.rem(shard + k, SHARDS)

    def z_peer(k):
        return lax.rem(z + k, nz)

    def y_peer(k):
        return lax.rem(y + k, NY)

    def along_y(k):
        return (z * NY + y_peer(k), shard)

    def along_x(k):
        return (dp, lax.rem(x + k, NX) * 2 + core)

    across_table = (4, 3, 5, 2, 6, 1, 7)
    across_z = [nz // 2]
    for k in range(nz // 2 - 1, 0, -1):
        across_z += [k, nz - k]
    across_y = (2, 1, 3)

    barrier = greet(
        [(dp, table_peer(k)) for k in range(1, SHARDS)]
        + [(z_peer(k) * NY + y, shard) for k in range(1, nz)]
        + [along_y(k) for k in range(1, NY)]
    )

    local = [(req_hbm, req_ref)]
    for g in range(2):
        part = pl.ds(pl.multiple_of(shard * 256 + g * 128, 128), 128)
        local.append((w_hbm.at[:, part], wout.at[x, core, g, z, y]))
    local += [
        (table_hbm, table_ref),
        (cot_hbm, cot_ref),
        (first_hbm, first_ref),
        (second_hbm, second_ref),
        (slot_hbm, slot_ref),
        (seg_hbm, seg_ref),
        (tally_hbm, tally_ref),
        (target_hbm, target_ref),
    ]
    local = [pltpu.make_async_copy(a, b, local_s.at[i]) for i, (a, b) in enumerate(local)]
    for copy in local:
        copy.start()

    pl.semaphore_wait(*barrier)

    started = []

    def start(copy):
        copy.start()
        started.append(copy)
        return copy

    def drain():
        for copy in started:
            copy.wait_send()
        started.clear()

    local[1].wait()
    local[2].wait()
    for k in across_z:
        q = z_peer(k)
        block = wout.at[x, core, :, z, y]
        start(remote(block, block, z_s.at[k], z_r.at[z], (q * NY + y, shard)))

    local[0].wait()
    lane = lax.broadcasted_iota(jnp.int32, (CAP, 128), 1) % 32
    deep = lax.broadcasted_iota(jnp.int32, (CAP, 128), 0)
    wide = jnp.zeros((SHARDS, 128), f32)
    for m in range(MICRO):
        spot = jnp.where(lane == deep + m * CAP, 1.0, 0.0).astype(bf16)
        wide = wide + dot(req_ref[m].astype(f32).astype(bf16), spot)
    mine = lax.broadcasted_iota(jnp.int32, (SHARDS, 128), 1) // 32 == lax.rem(shard, 4)
    wide = jnp.where(mine, wide.astype(jnp.int32), -1)
    for p in range(SHARDS):
        asked[p] = jnp.broadcast_to(wide[p : p + 1], (8, 128))
    for k in across_table:
        p = table_peer(k)
        start(remote(asked.at[p], held.at[shard], req_s.at[k], req_r.at[shard], (dp, p)))
    held[shard] = asked[shard]

    local[3].wait()
    for k in reversed(across_table):
        p = table_peer(k)
        remote(asked.at[p], held.at[p], req_s.at[k], req_r.at[p], (dp, p)).wait_recv()
    for group in range(2):
        rows = dot(slot_rows(held, group), table_ref[...], ((0,), (0,)))
        found[4 * group : 4 * group + 4] = rows.astype(bf16).reshape(4, MICRO, CAP, columns)
    for k in across_table:
        p = table_peer(k)
        start(remote(found.at[p], fetched.at[shard], fnd_s.at[k], fnd_r.at[shard], (dp, p)))
    fetched[shard] = found[shard]

    for copy in local[7:]:
        copy.wait()
    count = seg_ref.shape[2]
    slots = SHARDS * CAP
    collect, expand, share = [], [], []
    number = lax.broadcasted_iota(jnp.int32, (slots, count), 0)
    user = lax.broadcasted_iota(jnp.int32, (8, count), 0)
    causal = lax.broadcasted_iota(jnp.int32, (count, count), 0) >= lax.broadcasted_iota(
        jnp.int32, (count, count), 1
    )
    for m in range(MICRO):
        hot = jnp.where(number == slot_ref[m], 1.0, 0.0)
        collect.append(hot.astype(bf16))
        expand.append(jnp.transpose(hot).astype(bf16))
        belongs = jnp.where(user == seg_ref[m], 1.0, 0.0).astype(bf16)
        same = dot(belongs, belongs, ((0,), (0,)))
        history = jnp.sum(same, axis=1, keepdims=True)
        share.append(jnp.where(causal, same, 0.0) / history)

    i32 = jnp.int32
    live = lax.broadcasted_iota(i32, (DCAP, 64), 0) < tally_ref[...]
    aims = jnp.where(live, target_ref[...] + 1, 0).astype(f32).astype(bf16)
    lane = lax.broadcasted_iota(i32, (64, 64), 1)
    deep = lax.broadcasted_iota(i32, (64, 64), 0)
    here = jnp.where(deep == (lane // DCAP) * SHARDS + shard, 1.0, 0.0).astype(bf16)
    aims = dot(aims, here)
    lane = lax.broadcasted_iota(i32, (DCAP, 64), 1) % DCAP
    deep = lax.broadcasted_iota(i32, (DCAP, 64), 0)
    aims = jnp.sum(jnp.where(lane == deep, aims, 0.0), axis=0, keepdims=True).astype(i32) - 1
    number = lax.broadcasted_iota(i32, (128, 64), 0)
    pick = jnp.where(number == aims, 1.0, 0.0)
    tally = jnp.sum(pick, axis=1, keepdims=True)
    pick = pick.astype(bf16)
    lane = lax.broadcasted_iota(i32, (64, 64), 1)
    deep = lax.broadcasted_iota(i32, (64, 64), 0)
    limit = jnp.where(lane == shard * SHARDS + deep // DCAP, tally_ref[...].astype(f32), 0.0)
    limit = jnp.sum(limit, axis=1, keepdims=True)
    row = (lax.broadcasted_iota(i32, (64, 1), 0) % DCAP).astype(f32)
    scale = 1.0 / (1.0 + tally)
    scale = jnp.concatenate([scale[:64], jnp.where(row < limit, 0.0, scale[64:])], axis=0)

    for copy in local[4:7]:
        copy.wait()
    for p in range(SHARDS):
        line = slice(64 + DCAP * p, 64 + DCAP * p + DCAP)
        mom_send[p] = jnp.concatenate([first_ref[line], second_ref[line]], axis=0).astype(bf16)

    for k in reversed(across_z):
        q = z_peer(k)
        block = wout.at[x, core, :, q, y]
        remote(block, block, z_s.at[k], z_r.at[q], (q * NY + y, shard)).wait_recv()

    whole, low, high = pl.ds(0, nz), pl.ds(0, half), pl.ds(half, half)
    views = (
        lambda i, zs: wout.at[x, core, 0, zs, i],
        lambda i, zs: wout.at[i, core, 1, zs, y],
        lambda i, zs: wout.at[i, core, 0, zs],
        lambda i, zs: wout.at[:, core, 1, zs, i],
    )
    spots = (y, x, x, y)
    steps = (along_y, along_x, along_x, along_y)

    def link(ring, which, offset, zs, to):
        block = views[ring](lax.rem(spots[ring] + offset, 4), zs)
        return remote(
            block, block, ring_s.at[ring, which], ring_r.at[ring, which], steps[ring](to)
        )

    def ring_first(ring):
        start(link(ring, 0, 0, whole, 1))
        start(link(ring, 1, 0, whole, 3))

    def ring_second(ring):
        link(ring, 0, 3, whole, 1).wait_recv()
        start(link(ring, 2, 3, low, 1))
        link(ring, 1, 1, whole, 3).wait_recv()
        start(link(ring, 3, 1, high, 3))

    def ring_third(ring):
        link(ring, 2, 2, low, 1).wait_recv()
        link(ring, 3, 2, high, 3).wait_recv()

    def across(ring, offset, mine=True):
        i = lax.rem(spots[ring] + offset, 4)
        c = core if mine else other
        block = wout.at[i, c, 0] if ring == 2 else wout.at[:, c, 1, :, i]
        s = (ring - 2) * 4 + offset
        return remote(block, block, core_s.at[s], core_r.at[s], (dp, x * 2 + other))

    def middle(ring, which, offset):
        block = views[ring](lax.rem(spots[ring] + offset, 4), whole)
        return remote(
            block, block, ring_s.at[ring, which], ring_r.at[ring, which], steps[ring](which)
        )

    for which in (2, 1, 3):
        for ring in (0, 1):
            start(middle(ring, which, 0))
    for which in (1, 3, 2):
        for ring in (0, 1):
            middle(ring, which, 4 - which).wait_recv()
    for ring in (2, 3):
        ring_first(ring)
        start(across(ring, 0))

    for k in reversed(across_table):
        p = table_peer(k)
        remote(found.at[p], fetched.at[p], fnd_s.at[k], fnd_r.at[p], (dp, p)).wait_recv()
    rows = jnp.concatenate(
        [fetched[:, m].reshape(slots, columns) for m in range(MICRO)], axis=0
    ).astype(f32)
    normed, factor = normalise(rows)
    given = normed.astype(bf16)
    lane = lax.broadcasted_iota(jnp.int32, (1, columns), 1)
    deep = lax.broadcasted_iota(jnp.int32, (columns, 256), 0)
    for i in range(NY):
        j = lane[:, 256 * i : 256 * i + 256]
        origin = ((j // 16) % nz) * (NY * 16) + (j // (16 * nz)) * 16 + j % 16
        order = jnp.where(deep == origin, 1.0, 0.0).astype(bf16)
        given_y[:, 256 * i : 256 * i + 256] = dot(given, order).astype(bf16)

    def finish(flat, at):
        at = pl.ds(pl.multiple_of(at, 128), 128)
        sig = sigmoid(flat)
        slope[:, at] = sig * (1.0 + flat * (1.0 - sig))
        top = (flat * sig).astype(bf16)
        for m in range(MICRO):
            tokens_of = dot(expand[m], top[m * slots : (m + 1) * slots])
            flow[m * count : (m + 1) * count, at] = tokens_of.astype(bf16)

    def project_x(offset, c):
        i = lax.rem(x + offset, NX)
        finish(dot(given, wout[i, c, 0].reshape(columns, 128)), i * 512 + c * 256)

    def project_y(offset, which):
        i, c = y_peer(offset), (core, other)[which]
        block = jnp.concatenate([wout[n, c, 1, :, i].reshape(16 * nz, 128) for n in range(NX)], axis=1)
        mine = given_y[:, pl.ds(pl.multiple_of(i * 256, 256), 256)]
        if offset == 0:
            sums[which] = dot(mine, block)
        else:
            sums[which] += dot(mine, block)

    def project_rest(which):
        c = (core, other)[which]
        for n in range(NX):
            finish(sums[which, :, 128 * n : 128 * n + 128], n * 512 + c * 256 + 128)

    def project(offsets):
        for offset in offsets:
            project_x(offset, core)
            project_y(offset, 0)
        if offsets[-1] == 2:
            project_rest(0)
        for offset in offsets:
            for ring in (2, 3):
                across(ring, offset, mine=False).wait_recv()
            project_x(offset, other)
            project_y(offset, 1)
        if offsets[-1] == 2:
            project_rest(1)

    project((0,))
    for ring in (2, 3):
        ring_second(ring)
        start(across(ring, 3))
        start(across(ring, 1))
    project((3, 1))

    for ring in (2, 3):
        ring_third(ring)
        start(across(ring, 2))

    project((2,))
    for k in across_table:
        p = table_peer(k)
        start(remote(mom_send.at[p], mom_got.at[shard], m_s.at[k], m_r.at[shard], (dp, p)))
    mom_got[shard] = mom_send[shard]

    width = 512
    head = width // HEADS

    def weight(i):
        sides = [wout[i // 2, i % 2, g].reshape(columns, 128) for g in range(2)]
        return jnp.concatenate(sides, axis=1)

    def slot_send(piece, src, to, k, p):
        m = min(piece, 1)
        over = slice(None) if piece == 0 else pl.ds((piece - 1) * columns // 2, columns // 2)
        return remote(
            grads.at[src, m, :, over],
            arrived.at[to, m, :, over],
            a_s.at[piece, k],
            a_r.at[piece, to],
            (dp, p),
        )

    factor_scale = head ** (-0.5)
    for m in range(MICRO):
        span = slice(m * count, (m + 1) * count)
        part = slice(m * slots, (m + 1) * slots)
        for h in range(HEADS):
            values = flow[span, width + h * head : width + (h + 1) * head]
            queries = flow[span, 2 * width + h * head : 2 * width + (h + 1) * head]
            keys = flow[span, 3 * width + h * head : 3 * width + (h + 1) * head]
            scores = dot(queries, keys, ((1,), (1,))) * factor_scale
            sig = sigmoid(scores)
            shared = share[m] * sig
            weights = (scores * shared).astype(bf16)
            attn[h] = weights
            attn_slope[h] = shared * (1.0 + scores * (1.0 - sig)) * factor_scale
            mixed[:, h * head : (h + 1) * head] = dot(weights, values)
        level, spread = normalise(mixed[...])
        upstream = cot_ref[m].astype(f32)
        back[:, :width] = (upstream * level).astype(bf16)
        grad_mixed = normalise_back(
            upstream * flow[span, :width].astype(f32), level, spread
        ).astype(bf16)
        for h in range(HEADS):
            values = flow[span, width + h * head : width + (h + 1) * head]
            queries = flow[span, 2 * width + h * head : 2 * width + (h + 1) * head]
            keys = flow[span, 3 * width + h * head : 3 * width + (h + 1) * head]
            grad_out = grad_mixed[:, h * head : (h + 1) * head]
            grad_attn = dot(grad_out, values, ((1,), (1,))).astype(bf16)
            grad_scores = (grad_attn.astype(f32) * attn_slope[h]).astype(bf16)
            at = width + h * head
            back[:, at : at + head] = dot(attn[h], grad_out, ((0,), (0,))).astype(bf16)
            at = 2 * width + h * head
            back[:, at : at + head] = dot(grad_scores, keys).astype(bf16)
            at = 3 * width + h * head
            back[:, at : at + head] = dot(grad_scores, queries, ((0,), (0,))).astype(bf16)
        grad_normed = jnp.zeros((slots, columns), f32)
        for i in range(8):
            side = slice(256 * i, 256 * i + 256)
            grad_flat = (dot(collect[m], back[:, side]) * slope[part, side]).astype(bf16)
            grad_normed = grad_normed + dot(grad_flat, weight(i), ((1,), (1,)))
        grad_normed = grad_normed.astype(bf16).astype(f32)
        slot_grad = normalise_back(grad_normed, normed[part], factor[part]).astype(bf16)
        grads[:, m] = slot_grad.reshape(SHARDS, CAP, columns)
        for piece in ((0,), (1, 2))[m]:
            for k in across_table:
                start(slot_send(piece, table_peer(k), shard, k, table_peer(k)))
    arrived[shard] = grads[shard]

    asks = [slot_rows(held, group) for group in range(2)]
    side = columns // 2
    tiles = nz // 2
    lines = blocks // 2

    def half_sums(h):
        for piece in ((0, 1), (2,))[h]:
            for k in reversed(across_table):
                p = table_peer(k)
                slot_send(piece, p, p, k, p).wait_recv()
        dense = jnp.zeros((128, side), f32)
        for group in range(2):
            came = arrived[4 * group : 4 * group + 4, :, :, h * side : (h + 1) * side]
            dense = dense + dot(asks[group], came.reshape(128, side))
        dense = dense.astype(bf16)
        for part in range(NY):
            for r in range(2):
                for b in range(lines):
                    at = part * 32 + r * 16
                    y_send[part, h * tiles + r * lines + b] = dense[
                        at : at + 16, b * 128 : b * 128 + 128
                    ]

    def half_y(h, q, to, k):
        part = pl.ds(h * tiles, tiles)
        return remote(
            y_send.at[q, part], y_got.at[to, part], ry_s.at[h, k], ry_r.at[h, to], along_y(k)
        )

    def half_z(h, j):
        q = lax.rem(z + j, tiles) + h * tiles
        return remote(z_send.at[q], z_got.at[z], rz_s.at[h, j], rz_r.at[z], (q * NY + y, shard))

    around = [tiles // 2]
    for j in range(tiles // 2 - 1, 0, -1):
        around += [j, tiles - j]

    for h in range(2):
        half_sums(h)
        for k in across_y:
            start(half_y(h, y_peer(k), y, k))
    drain()
    for h in range(2):
        part = slice(h * tiles, (h + 1) * tiles)
        y_sum = y_send[y, part].astype(f32)
        for k in reversed(across_y):
            q = y_peer(k)
            half_y(h, q, q, k).wait_recv()
            y_sum = y_sum + y_got[q, part].astype(f32)
        z_send[part] = y_sum.astype(bf16)
        for j in around:
            start(half_z(h, j))

        @pl.when(z // tiles != h)
        def _():
            half_z(h, 0).start()

    z_sum = z_send[z].astype(f32)
    for k in reversed(across_z):
        q = z_peer(k)
        remote(z_send.at[q], z_got.at[q], rz_s.at[0, 0], rz_r.at[q], (q * NY + y, shard)).wait_recv()
        z_sum = z_sum + z_got[q].astype(f32)
    total[y, z] = z_sum.astype(bf16)

    for k in across_z:
        q = z_peer(k)
        block = total.at[y, z]
        start(remote(block, block, gz_s.at[k], gz_r.at[z], (q * NY + y, shard)))
    def tile_of(q):
        block = total.at[y, q]
        return remote(block, block, gz_s.at[1], gz_r.at[q], (q * NY + y, shard))

    def out_y(h, q, k):
        block = total.at[q, pl.ds(h * tiles, tiles)]
        return remote(block, block, gy_s.at[h, k], gy_r.at[h, q], along_y(k))

    for h in range(2):
        for j in reversed(around):
            tile_of(lax.rem(z + j, tiles) + h * tiles).wait_recv()

        @pl.when(z // tiles != h)
        def _():
            tile_of(lax.rem(z, tiles) + h * tiles).wait_recv()

        for k in across_y:
            start(out_y(h, y, k))

    for k in reversed(across_table):
        p = table_peer(k)
        remote(mom_send.at[p], mom_got.at[p], m_s.at[k], m_r.at[p], (dp, p)).wait_recv()
    def rep_out(h, src, to, k, p):
        return remote(
            rep_send.at[h, src], rep_got.at[h, to], r_s.at[h, k], r_r.at[h, to], (dp, p)
        )

    for h in range(2):
        for k in reversed(across_y):
            out_y(h, y_peer(k), k).wait_recv()
        grad = [
            jnp.concatenate(
                [total[n // 2, h * tiles + (n % 2) * lines + b] for b in range(lines)], axis=1
            ).astype(f32)
            for n in range(8)
        ]
        for p in range(SHARDS):
            own = grad[4 + p // 2][(p % 2) * 8 : (p % 2) * 8 + 8]
            rep_send[h, p] = jnp.concatenate(
                [own[:, : side // 2], own[:, side // 2 :]], axis=0
            ).astype(bf16)
        for k in across_table:
            p = table_peer(k)
            start(rep_out(h, p, shard, k, p))
        rep_got[h, shard] = rep_send[h, shard]
        over = slice(h * side, (h + 1) * side)
        for n in range(8):
            span = slice(16 * n, 16 * n + 16)
            first_out[span, over] = beta_one * first_ref[span, over] + (1.0 - beta_one) * grad[n]
            second_out[span, over] = beta_two * second_ref[span, over] + (1.0 - beta_two) * (
                grad[n] * grad[n]
            )
    drain()
    for h in range(2):
        over = slice(h * side, (h + 1) * side)
        for k in reversed(across_table):
            p = table_peer(k)
            rep_out(h, p, p, k, p).wait_recv()
        rep_first, rep_second = [], []
        for p in range(SHARDS):
            halves = rep_got[h, p].astype(f32)
            grad = jnp.concatenate([halves[:8], halves[8:]], axis=1)
            moments = mom_got[p, :, over].astype(f32)
            rep_first.append(beta_one * moments[:8] + (1.0 - beta_one) * grad)
            rep_second.append(beta_two * moments[8:] + (1.0 - beta_two) * (grad * grad))
        rep_first = dot(pick, jnp.concatenate(rep_first, axis=0).astype(bf16))
        rep_second = dot(pick, jnp.concatenate(rep_second, axis=0).astype(bf16))
        first_out[:, over] = (first_out[:, over] + rep_first) * scale
        second_out[:, over] = (second_out[:, over] + rep_second) * scale
    for h in range(2):

        @pl.when(z // tiles != h)
        def _():
            half_z(h, 0).wait_send()

    for copy in started:
        copy.wait_send()


def body(
    nz,
    token_slot,
    seg_ids,
    req_rows,
    cotangent,
    uvqk_weight,
    table,
    first_moment,
    second_moment,
    dup_count,
    dup_target,
):
    columns = table.shape[1]
    count = token_slot.shape[2]
    tokens = MICRO * count
    slots = SHARDS * CAP
    vmem = pl.BlockSpec(memory_space=pltpu.VMEM)
    hbm = pl.BlockSpec(memory_space=pl.ANY)
    dma = pltpu.SemaphoreType.DMA
    bf16, f32, i32 = jnp.bfloat16, jnp.float32, jnp.int32

    tiles = 2 * columns // 128
    first, second = pl.pallas_call(
        functools.partial(whole_kernel, nz),
        out_shape=(
            jax.ShapeDtypeStruct(table.shape, f32),
            jax.ShapeDtypeStruct(table.shape, f32),
        ),
        in_specs=[hbm] * 10,
        out_specs=(vmem,) * 2,
        scratch_shapes=[
            pltpu.VMEM(req_rows.shape, i32),
            pltpu.VMEM(token_slot.shape, i32),
            pltpu.VMEM(seg_ids.shape, i32),
            pltpu.VMEM((1, SHARDS * SHARDS), i32),
            pltpu.VMEM((DCAP, SHARDS * SHARDS), i32),
            pltpu.VMEM((SHARDS, 8, 128), i32),
            pltpu.VMEM((SHARDS, 8, 128), i32),
            pltpu.VMEM(table.shape, bf16),
            pltpu.VMEM((NX, 2, 2, nz, NY, 16, 128), bf16),
            pltpu.VMEM((MICRO, count, 512), bf16),
            pltpu.VMEM(table.shape, f32),
            pltpu.VMEM(table.shape, f32),
            pltpu.VMEM((SHARDS, MICRO, CAP, columns), bf16),
            pltpu.VMEM((SHARDS, MICRO, CAP, columns), bf16),
            pltpu.VMEM((MICRO * slots, columns), bf16),
            pltpu.VMEM((2, MICRO * slots, 512), f32),
            pltpu.VMEM((MICRO * slots, 2048), f32),
            pltpu.VMEM((tokens, 2048), bf16),
            pltpu.VMEM((HEADS, count, count), bf16),
            pltpu.VMEM((HEADS, count, count), f32),
            pltpu.VMEM((count, 512), f32),
            pltpu.VMEM((count, 2048), bf16),
            pltpu.VMEM((SHARDS, MICRO, CAP, columns), bf16),
            pltpu.VMEM((SHARDS, MICRO, CAP, columns), bf16),
            pltpu.VMEM((NY, tiles, 16, 128), bf16),
            pltpu.VMEM((NY, tiles, 16, 128), bf16),
            pltpu.VMEM((tiles, 16, 128), bf16),
            pltpu.VMEM((tiles, 16, 128), bf16),
            pltpu.VMEM((NY, tiles, 16, 128), bf16),
            pltpu.VMEM((SHARDS, 16, columns), bf16),
            pltpu.VMEM((SHARDS, 16, columns), bf16),
            pltpu.VMEM((2, SHARDS, 16, columns // 4), bf16),
            pltpu.VMEM((2, SHARDS, 16, columns // 4), bf16),
            dma((11,)),
            dma((SHARDS,)),
            dma((SHARDS,)),
            dma((SHARDS,)),
            dma((SHARDS,)),
            dma((nz,)),
            dma((nz,)),
            dma((4, 4)),
            dma((4, 4)),
            dma((8,)),
            dma((8,)),
            dma((3, SHARDS)),
            dma((3, SHARDS)),
            dma((2, NY)),
            dma((2, NY)),
            dma((2, nz // 2)),
            dma((nz,)),
            dma((nz,)),
            dma((nz,)),
            dma((2, NY)),
            dma((2, NY)),
            dma((SHARDS,)),
            dma((SHARDS,)),
            dma((2, SHARDS)),
            dma((2, SHARDS)),
        ],
        compiler_params=pltpu.CompilerParams(
            collective_id=0, has_side_effects=True, vmem_limit_bytes=63 << 20
        ),
        name="whole",
    )(
        req_rows,
        token_slot,
        seg_ids,
        dup_count[None, :],
        dup_target.T,
        table,
        uvqk_weight,
        cotangent,
        first_moment,
        second_moment,
    )
    keep = second > 0.0
    new_first = jnp.where(keep, first, 0.0)
    new_second = jnp.where(keep, second, 0.0)
    update = table.astype(f32) - learn_rate * new_first / (jnp.sqrt(new_second) + adam_eps)
    return (jnp.where(keep, update, 0.0).astype(bf16), new_first, new_second)


def solution(mesh):
    placed = (
        P(None, ("dp", "table"), None),
        P(None, ("dp", "table"), None),
        P(None, ("dp", "table"), None),
        P(None, ("dp", "table"), None),
        P("dp", None),
        P("table", None),
        P("table", None),
        P("table", None),
        P(),
        P(),
    )
    return jax.shard_map(
        functools.partial(body, mesh.shape["dp"] // NY),
        mesh=mesh,
        in_specs=placed,
        out_specs=(P("table", None), P("table", None), P("table", None)),
        check_vma=False,
    )
```
